32 devices in a mesh: wide: 8 (over z, y), narrow: 4 (over x, core).
Axes of the slice: x: 2, y: 2, z: 4, core: 2. Of those that a mesh axis runs over, the one named last changes fastest.
Arguments:
- boards: float32 [384, 8, 8, 256], P(('wide', 'narrow'))
- history_mask: int32 [384, 8], P(('wide', 'narrow')), may hold values 0 or 1
- kernels: float32 [2, 256, 2304], replicated, may hold values from -0.125 to 0.125
- norm_params: float32 [2, 2, 256], replicated, as said below
- norm_momenta: float32 [2, 2, 256], replicated
- left_stats: float32 [2, 256, 256], replicated
- right_stats: float32 [2, 2304, 2304], P(None, None, 'narrow')
- left_roots: float32 [2, 256, 256], replicated
- right_roots: float32 [2, 2304, 2304], P(None, None, 'narrow')
- out_cotangent: float32 [384, 8, 8, 256], P(('wide', 'narrow'))
Outputs:
- block_out: float32 [384, 8, 8, 256], P(('wide', 'narrow'))
- board_grad: float32 [384, 8, 8, 256], P(('wide', 'narrow'))
- kernel_grad: float32 [2, 256, 2304], P(None, None, 'narrow')
- new_kernels: float32 [2, 256, 2304], P(None, None, 'narrow')
- new_left: float32 [2, 256, 256], replicated
- new_right: float32 [2, 2304, 2304], P(None, None, 'narrow')
- new_momenta: float32 [2, 2, 256], replicated
- new_norm_params: float32 [2, 2, 256], replicated
The draws below stay inside these ranges and needn't reach their ends.
Inputs may be any that keep to these rules, and one draw needn't show every extreme that they name: `norm_params`: gains positive.
All inputs are finite; a program needn't handle non-finite values. No bound on the sum of `history_mask` on one device may be relied on, other than what follows from the above.
Results may differ from the reference program's by a relative error of at most 0.012.
Values sent between devices are 32-bit elements; how exact they have to be, the bound alone decides.
A program may use at most 128 MiB of HBM per device.

```python
import math
import jax
import jax.numpy as jnp
from jax import lax

C = 256
HIST = 8
P_DEV = 12
KIN = 2304
POSITIONS = 384
N_WIDE = 8
N_NARROW = 4


def row_scale(key, base, rise):
    positions = jnp.arange(POSITIONS)
    device = positions // P_DEV
    wide_pos = (device // N_NARROW).astype(jnp.float32)
    narrow_pos = (device % N_NARROW).astype(jnp.float32)
    wide_frac = wide_pos / max(N_WIDE - 1, 1)
    narrow_frac = narrow_pos / max(N_NARROW - 1, 1)
    rough = jnp.exp(math.log(2.0) * jax.random.uniform(key, (POSITIONS,), jnp.float32))
    return base * jnp.power(rise, wide_frac + narrow_frac) * rough


def board_field(key, base, rise, offset_size):
    key_noise, key_rows, key_offset = jax.random.split(key, 3)
    noise = jnp.clip(jax.random.normal(key_noise, (POSITIONS, 8, 8, C), jnp.float32), -4.0, 4.0)
    offset = offset_size * jnp.clip(jax.random.normal(key_offset, (C,), jnp.float32), -3.0, 3.0)
    scale = row_scale(key_rows, base, rise)
    return scale[:, None, None, None] * (noise + offset)


def draw_boards(key, part):
    key = jax.random.fold_in(key, 11)
    return board_field(key, 0.3, 3.0, 0.5)


def draw_out_cotangent(key, part):
    key = jax.random.fold_in(key, 12)
    return board_field(key, 0.3, 3.0, 0.0)


def draw_norm_params(key, part):
    key = jax.random.fold_in(key, 13)
    key_gain, key_shift = jax.random.split(key)
    gains = jax.random.uniform(key_gain, (2, C), jnp.float32, 0.7, 1.3)
    shifts = 0.5 * jnp.clip(jax.random.normal(key_shift, (2, C), jnp.float32), -3.0, 3.0)
    return jnp.stack([gains, shifts], axis=1)


def draw_norm_momenta(key, part):
    key = jax.random.fold_in(key, 14)
    grad_size = float(POSITIONS * 64) ** (-0.5)
    return grad_size * jnp.clip(jax.random.normal(key, (2, 2, C), jnp.float32), -4.0, 4.0)


def stat_matrix(key, size, base):
    key_diag, key_off = jax.random.split(key)
    diagonal = base * jnp.exp(math.log(4.0) * jax.random.uniform(key_diag, (2, size), jnp.float32))
    off = jnp.clip(jax.random.normal(key_off, (2, size, size), jnp.float32), -4.0, 4.0)
    identity = jnp.eye(size, dtype=jnp.float32)
    return diagonal[:, :, None] * identity + 0.5 * base / math.sqrt(size) * off


def draw_left_stats(key, part):
    key = jax.random.fold_in(key, 15)
    base = KIN / float(POSITIONS * 64)
    return stat_matrix(key, C, base)


def draw_right_stats(key, part):
    key = jax.random.fold_in(key, 16)
    base = C / float(POSITIONS * 64)
    return stat_matrix(key, KIN, base)


def draw_left_roots(key, part):
    key = jax.random.fold_in(key, 17)
    base = (KIN / float(POSITIONS * 64)) ** (-0.25)
    return stat_matrix(key, C, base)


def draw_right_roots(key, part):
    key = jax.random.fold_in(key, 18)
    base = (C / float(POSITIONS * 64)) ** (-0.25)
    return stat_matrix(key, KIN, base)


def with_ends(result, key, least, largest):
    dims = result.shape
    index_at = [jax.random.randint(jax.random.fold_in(key, axis), (), 0, dims[axis]) for axis in range(len(dims))]
    result = result.at[tuple(index_at)].set(least)
    longest = dims.index(max(dims))
    index_at[longest] = (index_at[longest] + 1) % dims[longest]
    return result.at[tuple(index_at)].set(largest)


def centred(own_key, shape, scale, limit, held_as=jnp.bfloat16):
    result = scale * jax.random.normal(own_key, shape, jnp.float32)
    return jnp.clip(result, min=-limit, max=limit).astype(held_as)


def setup_inputs(seed: int = 0) -> dict:
    arg_keys = jax.random.split(jax.random.key(seed), 11)
    boards = draw_boards(jax.random.fold_in(arg_keys[10], 71), 0)
    history_mask = with_ends((jax.random.randint(arg_keys[1], (POSITIONS, HIST), 0, 4) < 3).astype(jnp.int32), jax.random.fold_in(arg_keys[1], 1), 0, 1)
    kernels = centred(arg_keys[2], (2, C, KIN), KIN ** -0.5, 0.125, jnp.float32)
    norm_params = draw_norm_params(jax.random.fold_in(arg_keys[10], 71), 0)
    norm_momenta = draw_norm_momenta(jax.random.fold_in(arg_keys[10], 71), 0)
    left_stats = draw_left_stats(jax.random.fold_in(arg_keys[10], 71), 0)
    right_stats = draw_right_stats(jax.random.fold_in(arg_keys[10], 71), 0)
    left_roots = draw_left_roots(jax.random.fold_in(arg_keys[10], 71), 0)
    right_roots = draw_right_roots(jax.random.fold_in(arg_keys[10], 71), 0)
    out_cotangent = draw_out_cotangent(jax.random.fold_in(arg_keys[10], 71), 0)
    return dict(boards=boards, history_mask=history_mask, kernels=kernels, norm_params=norm_params, norm_momenta=norm_momenta, left_stats=left_stats, right_stats=right_stats, left_roots=left_roots, right_roots=right_roots, out_cotangent=out_cotangent)


EPS = 1e-05
MOMENTUM = 0.9
NORM_RATE = 50.0
KERNEL_RATE = 0.1
STAT_DECAY = 0.5

@jax.custom_vjp
def low(v):
    return lax.optimization_barrier(v.astype(jnp.bfloat16)).astype(jnp.float32)

@jax.custom_vjp
def low_back(v):
    return v

def low_keep(v):
    return (low(v), None)

def low_pass(kept, grad):
    return (grad,)

def back_keep(v):
    return (v, None)

def back_low(kept, grad):
    return (low(grad),)
low.defvjp(low_keep, low_pass)
low_back.defvjp(back_keep, back_low)

def convolve(boards_in, kernel):
    out_count = kernel.shape[0]
    in_count = boards_in.shape[3]
    filters = kernel.reshape(out_count, 3, 3, in_count).transpose(1, 2, 3, 0)
    return lax.conv_general_dilated(boards_in, filters, (1, 1), 'SAME', dimension_numbers=('NHWC', 'HWIO', 'NHWC'), precision=lax.Precision.HIGHEST)

def batch_norm(conv_out, gain, shift):
    mean_val = lax.optimization_barrier(jnp.mean(conv_out, axis=(0, 1, 2)))
    variance = lax.optimization_barrier(jnp.mean(jnp.square(conv_out - mean_val), axis=(0, 1, 2)))
    return (conv_out - mean_val) * lax.rsqrt(variance + EPS) * gain + shift

def forward(masked, kernels, norm_params):
    conv_one = low_back(convolve(low(masked), low(kernels[0])))
    hidden = jax.nn.gelu(batch_norm(conv_one, norm_params[0, 0], norm_params[0, 1]))
    conv_two = low_back(convolve(low(hidden), low(kernels[1])))
    summed = masked + batch_norm(conv_two, norm_params[1, 0], norm_params[1, 1])
    return jax.nn.gelu(summed)

def reference(boards, history_mask, kernels, norm_params, norm_momenta, left_stats, right_stats, left_roots, right_roots, out_cotangent):
    planes = jnp.repeat(history_mask.astype(jnp.float32), C // HIST, axis=1)[:, None, None, :]
    masked = boards * planes
    block_out, pull_back = jax.vjp(forward, masked, kernels, norm_params)
    d_masked, d_kernels, d_params = pull_back(out_cotangent)
    board_grad = d_masked * planes
    squares = float(POSITIONS * 64)
    kernel_grad = d_kernels / squares
    highest = lax.Precision.HIGHEST
    new_momenta = MOMENTUM * norm_momenta + d_params / squares
    new_norm_params = norm_params - NORM_RATE * new_momenta
    new_left = STAT_DECAY * left_stats + (1.0 - STAT_DECAY) * jnp.einsum('kab,kcb->kac', kernel_grad, kernel_grad, precision=highest)
    new_right = STAT_DECAY * right_stats + (1.0 - STAT_DECAY) * jnp.einsum('kba,kbc->kac', kernel_grad, kernel_grad, precision=highest)
    left_applied = jnp.einsum('kab,kbc->kac', left_roots, kernel_grad, precision=highest)
    update = jnp.einsum('kab,kbc->kac', left_applied, right_roots, precision=highest)
    new_kernels = kernels - KERNEL_RATE * update
    return (block_out, board_grad, kernel_grad, new_kernels, new_left, new_right, new_momenta, new_norm_params)
```

```python
import functools
import math

import jax
import jax.numpy as jnp
from jax import lax
from jax.experimental import pallas as pl
from jax.experimental.pallas import tpu as pltpu
from jax.sharding import PartitionSpec as P

EPS = 1e-05
MOMENTUM = 0.9
NORM_RATE = 50.0
KERNEL_RATE = 0.1
STAT_DECAY = 0.5

SIDE = 8
CUBE = 0.044715
ROOT = math.sqrt(2.0 / math.pi)
MESH = pl.DeviceIdType.MESH
F32 = jnp.float32
BF16 = jnp.bfloat16
MIB = 2**20


def dot(lhs, rhs, lhs_dim, rhs_dim):
    return lax.dot_general(
        lhs, rhs, (((lhs_dim,), (rhs_dim,)), ((), ())), preferred_element_type=F32
    )


def gelu_tanh(v):
    return jnp.tanh(ROOT * (v + CUBE * (v * v * v)))


def gelu_slope(v, t):
    inner = ROOT * (1.0 + (3.0 * CUBE) * (v * v))
    return 0.5 * (1.0 + t) + (0.5 * v) * ((1.0 - t * t) * inner)


def flip(index, bit):
    return index + (1 - 2 * ((index // (1 << bit)) % 2)) * (1 << bit)


def bit_of(index, bit):
    return (index // (1 << bit)) % 2


def pick(taken, one, other):
    return taken * one + (1 - taken) * other


def fused_kernel(
    dims,
    boards,
    mask_t,
    kernels,
    params,
    momenta,
    left_stats,
    left_roots,
    right_stats,
    right_roots,
    cotangent,
    g_full,
    stats_v,
    roots_v,
    lstats_v,
    lroots_v,
    kt,
    bo,
    bg,
    new_momenta,
    new_params,
    bd,
    ct,
    mk,
    par,
    mom,
    kf,
    wb,
    ktmp,
    x_one,
    x_two,
    dgrid,
    h_one,
    slope_one,
    h_two,
    d_sum,
    d_hid,
    gp,
    red,
    half_in,
    first_in,
    second_in,
    depth_in,
    more_in,
    load_sem,
    red_send,
    red_recv,
    g_send,
    g_recv,
):
    nw, nn, pos, chan = dims
    line = pos * SIDE
    rows = line * SIDE
    count = float(rows * nw * nn)
    taps = 9 * chan
    chunk = 3 * chan
    part0, part1, part2, part3 = chunk // 2, chunk // 4, chunk // 8, chunk // 32
    wide, narrow = lax.axis_index("wide"), lax.axis_index("narrow")
    me = wide * nn + narrow
    extra_bits = list(range(3, nw.bit_length() - 1))

    def load(slot, src, dst):
        copy = pltpu.make_async_copy(src, dst, load_sem.at[slot])
        copy.start()
        return copy

    got_k0 = load(0, kernels.at[0], kf.at[0])
    got_mask = load(1, mask_t, mk)
    got_boards = [load(2 + i, boards.at[:, i], bd.at[i]) for i in range(SIDE)]
    got_par = load(10, params, par)

    def each_other(act):
        if nw * nn <= 32:
            for k in range(nw * nn - 1, 0, -1):
                w, n = wide, narrow
                for b in range(nw.bit_length() - 1):
                    if (k // nn) >> b & 1:
                        w = flip(w, b) if b == 0 else w + (flip(wide, b) - wide)
                for b in range(nn.bit_length() - 1):
                    if (k % nn) >> b & 1:
                        n = n + (flip(narrow, b) - narrow)
                act((w, n))
        else:

            @pl.loop(1, nw * nn)
            def _(k):
                other = lax.rem(me + k, nw * nn)
                act((other // nn, lax.rem(other, nn)))

    barrier = pltpu.get_barrier_semaphore()
    each_other(
        lambda dev: pl.semaphore_signal(barrier, inc=1, device_id=dev, device_id_type=MESH)
    )

    def share(slot, value):
        red[slot, me] = value

        def send(dev):
            pltpu.make_async_remote_copy(
                src_ref=red.at[slot, me],
                dst_ref=red.at[slot, me],
                send_sem=red_send.at[slot],
                recv_sem=red_recv.at[slot],
                device_id=dev,
                device_id_type=MESH,
            ).start()

        each_other(send)

    def collect(slot):
        others = red.at[slot, pl.ds(0, nw * nn - 1)]
        pltpu.make_async_copy(others, others, red_recv.at[slot]).wait()
        pltpu.make_async_copy(others, others, red_send.at[slot]).wait()
        return red[slot]

    def moments(slot):
        got = collect(slot)
        means, spreads = got[:, 0, :], got[:, 1, :]
        mean = jnp.sum(means, axis=0, keepdims=True) * (1.0 / (nw * nn))
        gap = means - mean
        spread = jnp.sum(spreads, axis=0, keepdims=True) + float(rows) * jnp.sum(
            gap * gap, axis=0, keepdims=True
        )
        return mean, lax.rsqrt(spread / count + EPS)

    def totals(slot):
        got = collect(slot)
        return (
            jnp.sum(got[:, 0, :], axis=0, keepdims=True),
            jnp.sum(got[:, 1, :], axis=0, keepdims=True),
        )

    def local_moments(ref):
        total = jnp.sum(ref[...], axis=0, keepdims=True)
        mean = total * (1.0 / rows)
        gap = ref[...] - mean
        return jnp.concatenate([mean, jnp.sum(gap * gap, axis=0, keepdims=True)], axis=0)

    column = lax.broadcasted_iota(jnp.int32, (pos, SIDE, chan), 1)

    def put_shifted(grid, i, value):
        cube = value.reshape(pos, SIDE, chan)
        before = jnp.where(column == 0, 0.0, pltpu.roll(cube, 1, 1))
        after = jnp.where(column == SIDE - 1, 0.0, pltpu.roll(cube, SIDE - 1, 1))
        at = pl.ds(pl.multiple_of((i + 1) * line, 16), line)
        grid[at, 0:chan] = before.reshape(line, chan).astype(BF16)
        grid[at, chan : 2 * chan] = value.astype(BF16)
        grid[at, 2 * chan : 3 * chan] = after.reshape(line, chan).astype(BF16)

    def at_line(i):
        return pl.ds(pl.multiple_of(i * line, 8), line)

    def conv(grid, k):
        return sum(
            dot(
                grid[a * line : a * line + rows, :],
                wb[k, :, a * chunk : (a + 1) * chunk],
                1,
                1,
            )
            for a in range(3)
        )

    def conv_back(grid, k):
        result = None
        for a in range(3):
            for b in range(3):
                tap = 3 * (2 - a) + (2 - b)
                term = dot(
                    grid[a * line : a * line + rows, b * chan : (b + 1) * chan],
                    wb[k, :, tap * chan : (tap + 1) * chan],
                    1,
                    0,
                )
                result = term if result is None else result + term
        return result

    core = bit_of(narrow, 0)
    x_bit, y_bit = bit_of(narrow, 1), bit_of(wide, 0)
    z_low, z_high = bit_of(wide, 1), bit_of(wide, 2)
    z_pos = z_low + 2 * z_high
    core_dev = (wide, flip(narrow, 0))
    x_dev = (wide, flip(narrow, 1))
    y_dev = (flip(wide, 0), narrow)
    first_dev = (pick(core, y_dev[0], x_dev[0]), pick(core, y_dev[1], x_dev[1]))
    second_dev = (pick(core, x_dev[0], y_dev[0]), pick(core, x_dev[1], y_dev[1]))
    first_bit, second_bit = pick(core, y_bit, x_bit), pick(core, x_bit, y_bit)

    def z_other(q):
        low = 1 - z_low if q & 1 else z_low
        high = 1 - z_high if q & 2 else z_high
        return low + 2 * high

    sends = []

    def remote(k, a, slot, src, dst, dev):
        copy = pltpu.make_async_remote_copy(
            src_ref=src,
            dst_ref=dst,
            send_sem=g_send.at[k, a, slot],
            recv_sem=g_recv.at[k, a, slot],
            device_id=dev,
            device_id_type=MESH,
        )
        copy.start()
        sends.append(copy)
        return copy

    def exchange(k, a):
        base = a * chunk
        off0 = base + core * part0
        off1 = off0 + first_bit * part1
        off2 = off1 + second_bit * part2
        off3 = off2 + z_pos * part3
        live = {}

        def at(start, size):
            return pl.ds(pl.multiple_of(start, 8), size)

        def begin():
            src = gp.at[k, at(base + (1 - core) * part0, part0)]
            live["c"] = remote(k, a, 0, src, half_in.at[k, a], core_dev)

        def after_core():
            live["c"].wait_recv()
            own = at(off0, part0)
            gp[k, own] = gp[k, own] + half_in[k, a]
            src = gp.at[k, at(off0 + (1 - first_bit) * part1, part1)]
            live["1"] = remote(k, a, 1, src, first_in.at[k, a], first_dev)

        def after_first():
            live["1"].wait_recv()
            own = at(off1, part1)
            gp[k, own] = gp[k, own] + first_in[k, a]
            src = gp.at[k, at(off1 + (1 - second_bit) * part2, part2)]
            live["2"] = remote(k, a, 2, src, second_in.at[k, a], second_dev)

        def after_second():
            live["2"].wait_recv()
            own = at(off2, part2)
            gp[k, own] = gp[k, own] + second_in[k, a]
            live["z"] = []
            for q in (3, 2, 1):
                other = z_other(q)
                dev = (wide + 2 * (other - z_pos), narrow)
                src = gp.at[k, at(off2 + other * part3, part3)]
                live["z"].append(remote(k, a, 2 + q, src, depth_in.at[k, a, q - 1], dev))

        def after_depth():
            for copy in live["z"]:
                copy.wait_recv()
            own = at(off3, part3)
            value = ((gp[k, own] + depth_in[k, a, 0]) + depth_in[k, a, 1]) + depth_in[k, a, 2]
            for e, b in enumerate(extra_bits):
                gp[k, own] = value
                copy = remote(
                    k, a, 12 + e, gp.at[k, own], more_in.at[k, a, e], (flip(wide, b), narrow)
                )
                copy.wait_recv()
                copy.wait_send()
                sends.pop()
                value = value + more_in[k, a, e]
            g_full[k, own] = value * (1.0 / count)
            live["gz"] = []
            for q in (3, 2, 1):
                dev = (wide + 2 * (z_other(q) - z_pos), narrow)
                live["gz"].append(
                    remote(k, a, 5 + q, g_full.at[k, own], g_full.at[k, own], dev)
                )

        def back_depth():
            for copy in live["gz"]:
                copy.wait_recv()
            ref = g_full.at[k, at(off2, part2)]
            live["g2"] = remote(k, a, 9, ref, ref, second_dev)

        def back_second():
            live["g2"].wait_recv()
            ref = g_full.at[k, at(off1, part1)]
            live["g1"] = remote(k, a, 10, ref, ref, first_dev)

        def back_first():
            live["g1"].wait_recv()
            ref = g_full.at[k, at(off0, part0)]
            live["gc"] = remote(k, a, 11, ref, ref, core_dev)

        def end():
            live["gc"].wait_recv()

        return [
            begin,
            after_core,
            after_first,
            after_second,
            after_depth,
            back_depth,
            back_second,
            back_first,
            end,
        ]

    events = {(k, a): exchange(k, a) for k in range(2) for a in range(3)}

    def do(k, step):
        for a in range(3):
            events[k, a][step]()

    empty = jnp.zeros((line, 3 * chan), BF16)
    for grid in (x_one, x_two, dgrid):
        grid[0:line, :] = empty
        grid[line + rows : 2 * line + rows, :] = empty

    got_mask.wait()
    hist = mk.shape[0]
    width = chan // hist
    spot = lax.broadcasted_iota(jnp.int32, (pos, line), 1)
    owner = SIDE * lax.broadcasted_iota(jnp.int32, (pos, line), 0)
    spread_pos = jnp.where((spot >= owner) & (spot < owner + SIDE), 1.0, 0.0).astype(BF16)
    spot = lax.broadcasted_iota(jnp.int32, (hist, chan), 1)
    owner = width * lax.broadcasted_iota(jnp.int32, (hist, chan), 0)
    spread_chan = jnp.where((spot >= owner) & (spot < owner + width), 1.0, 0.0).astype(BF16)
    by_row = dot(mk[...].astype(F32).astype(BF16), spread_pos, 1, 0).astype(BF16)
    planes = dot(by_row, spread_chan, 0, 0)

    got_k0.wait()
    wb[0] = kf[0].astype(BF16)
    got_k1 = load(11, kernels.at[1], kf.at[1])
    got_ct = [load(12 + i, cotangent.at[:, i], ct.at[i]) for i in range(SIDE)]
    for i in range(SIDE):
        got_boards[i].wait()
        value = bd[i].reshape(line, chan) * planes
        bd[i] = value.reshape(pos, SIDE, chan)
        put_shifted(x_one, i, value)

    h_one[...] = conv(x_one, 0)
    local = local_moments(h_one)
    pl.semaphore_wait(barrier, nw * nn - 1)
    share(0, local)

    got_par.wait()
    late = [
        load(20, momenta, mom),
        load(21, left_stats, lstats_v),
        load(22, left_roots, lroots_v),
        load(23, right_roots, roots_v),
        load(24, right_stats, stats_v),
    ]
    got_k1.wait()
    wb[1] = kf[1].astype(BF16)

    def keep_share(k):
        share_width = kt.shape[1]
        span = ktmp.shape[0]
        start = narrow * share_width
        block = (start // 128) * 128
        ktmp[...] = kf[k, :, pl.ds(pl.multiple_of(block, 128), span)].T
        kt[k] = ktmp[pl.ds(pl.multiple_of(start - block, 8), share_width), :]

    keep_share(0)
    keep_share(1)

    gain_one, shift_one = par[0, 0:1, :], par[0, 1:2, :]
    gain_two, shift_two = par[1, 0:1, :], par[1, 1:2, :]

    mean_one, inv_one = moments(0)

    @pl.loop(0, SIDE)
    def _(i):
        at = at_line(i)
        normed = (h_one[at, :] - mean_one) * inv_one
        h_one[at, :] = normed
        pre = normed * gain_one + shift_one
        put_shifted(x_two, i, (0.5 * pre) * (1.0 + gelu_tanh(pre)))

    h_two[...] = conv(x_two, 1)
    share(1, local_moments(h_two))

    @pl.loop(0, SIDE)
    def _(i):
        at = at_line(i)
        pre = h_one[at, :] * gain_one + shift_one
        slope_one[at, :] = gelu_slope(pre, gelu_tanh(pre))

    for copy in got_ct:
        copy.wait()
    mean_two, inv_two = moments(1)

    def fold(value):
        return jnp.sum(value.reshape(pos, SIDE, chan), axis=0)

    nothing = jnp.zeros((SIDE, chan), F32)

    def close(gain_sum, shift_sum):
        return jnp.concatenate(
            [
                jnp.sum(gain_sum, axis=0, keepdims=True),
                jnp.sum(shift_sum, axis=0, keepdims=True),
            ],
            axis=0,
        )

    def out_line(i, carry):
        at = at_line(i)
        normed = (h_two[at, :] - mean_two) * inv_two
        h_two[at, :] = normed
        summed = bd[i].reshape(line, chan) + normed * gain_two + shift_two
        t = gelu_tanh(summed)
        bo[i] = ((0.5 * summed) * (1.0 + t)).reshape(pos, SIDE, chan)
        slope = ct[i].reshape(line, chan) * gelu_slope(summed, t)
        d_sum[at, :] = slope
        return carry[0] + fold(slope * normed), carry[1] + fold(slope)

    share(2, close(*lax.fori_loop(0, SIDE, out_line, (nothing, nothing))))

    gain_two_sum, shift_two_sum = totals(2)
    scale_two = gain_two * inv_two

    @pl.loop(0, SIDE)
    def _(i):
        at = at_line(i)
        lost = (shift_two_sum + h_two[at, :] * gain_two_sum) * (1.0 / count)
        put_shifted(dgrid, i, scale_two * (d_sum[at, :] - lost))

    def weight_chunk(grid, k, a):
        gp[k, a * chunk : (a + 1) * chunk, :] = dot(
            grid[a * line : a * line + rows, :], dgrid[line : line + rows, chan : 2 * chan], 0, 0
        )
        events[k, a][0]()

    for a in range(3):
        weight_chunk(x_two, 1, a)
    d_hid[...] = conv_back(dgrid, 1)
    do(1, 1)

    def pre_line(i, carry):
        at = at_line(i)
        d_pre = d_hid[at, :] * slope_one[at, :]
        d_hid[at, :] = d_pre
        return carry[0] + fold(d_pre * h_one[at, :]), carry[1] + fold(d_pre)

    share(3, close(*lax.fori_loop(0, SIDE, pre_line, (nothing, nothing))))
    gain_one_sum, shift_one_sum = totals(3)
    scale_one = gain_one * inv_one

    @pl.loop(0, SIDE)
    def _(i):
        at = at_line(i)
        lost = (shift_one_sum + h_one[at, :] * gain_one_sum) * (1.0 / count)
        put_shifted(dgrid, i, scale_one * (d_hid[at, :] - lost))

    for a in range(3):
        weight_chunk(x_one, 0, a)
    do(1, 2)
    d_hid[...] = conv_back(dgrid, 0)
    do(0, 1)
    for i in range(SIDE):
        at = at_line(i)
        bg[i] = ((d_sum[at, :] + d_hid[at, :]) * planes).reshape(pos, SIDE, chan)

    for copy in late:
        copy.wait()
    norm_grad = [
        jnp.concatenate([gain_one_sum, shift_one_sum], axis=0),
        jnp.concatenate([gain_two_sum, shift_two_sum], axis=0),
    ]
    for k in range(2):
        value = MOMENTUM * mom[k] + norm_grad[k] * (1.0 / count)
        new_momenta[k] = value
        new_params[k] = par[k] - NORM_RATE * value

    do(1, 3)
    do(0, 2)
    do(1, 4)
    do(0, 3)
    do(1, 5)
    do(0, 4)
    do(1, 6)
    do(0, 5)
    do(1, 7)
    do(0, 6)
    do(1, 8)
    do(0, 7)
    do(0, 8)
    for copy in sends:
        copy.wait_send()


def finish_kernel(
    dims,
    g_full,
    stats,
    roots,
    lstats,
    lroots,
    kt,
    bo,
    bg,
    momenta,
    params,
    o_block,
    o_board,
    o_grad,
    o_kernel,
    o_left,
    o_right,
    o_momenta,
    o_params,
    gb,
    nr,
    nk,
    nl,
    sem,
):
    chan = dims[3]
    chunk = 3 * chan
    share_width = kt.shape[1]
    start = pl.multiple_of(lax.axis_index("narrow") * share_width, 8)
    copies = []

    def put(src, dst):
        copy = pltpu.make_async_copy(src, dst, sem.at[len(copies)])
        copy.start()
        copies.append(copy)

    for k in range(2):
        put(g_full.at[k, pl.ds(start, share_width)], o_grad.at[k])
        gb[k] = g_full[k].astype(BF16)
        own = g_full[k, pl.ds(start, share_width), :].astype(BF16)
        for q in range(3):
            cols = pl.ds(q * chunk, chunk)
            term = dot(own, gb[k, cols, :], 1, 1)
            nr[k, q] = STAT_DECAY * stats[k, :, cols] + (1.0 - STAT_DECAY) * term
            put(nr.at[k, q], o_right.at[k, :, cols])
        if k == 0:
            for i in range(SIDE):
                put(bo.at[i], o_block.at[:, i])
                put(bg.at[i], o_board.at[:, i])
            put(momenta, o_momenta)
            put(params, o_params)
    for k in range(2):
        term = dot(gb[k], gb[k], 0, 0)
        nl[k] = STAT_DECAY * lstats[k] + (1.0 - STAT_DECAY) * term
        put(nl.at[k], o_left.at[k])
        mixed = dot(roots[k].astype(BF16), gb[k], 1, 0)
        update = dot(mixed.astype(BF16), lroots[k].astype(BF16), 1, 1)
        nk[k] = kt[k] - KERNEL_RATE * update
        put(nk.at[k], o_kernel.at[k])
    for copy in copies:
        copy.wait()


def body(
    nw,
    nn,
    boards,
    history_mask,
    kernels,
    norm_params,
    norm_momenta,
    left_stats,
    right_stats,
    left_roots,
    right_roots,
    out_cotangent,
):
    pos, chan = boards.shape[0], boards.shape[3]
    kin = kernels.shape[2]
    share_width = right_stats.shape[2]
    line = pos * SIDE
    rows = line * SIDE
    chunk = 3 * chan
    ndev = nw * nn
    extra = max(nw.bit_length() - 4, 0)
    dims = (nw, nn, pos, chan)
    hbm = pl.BlockSpec(memory_space=pl.ANY)
    vmem = pl.BlockSpec(memory_space=pltpu.VMEM)
    span = -(-(share_width + 64) // 128) * 128
    board_shape = (SIDE, pos, SIDE, chan)

    kept = [
        (2, kin, chan),
        (2, share_width, kin),
        (2, share_width, kin),
        (2, chan, chan),
        (2, chan, chan),
        (2, share_width, chan),
        board_shape,
        board_shape,
        (2, 2, chan),
        (2, 2, chan),
    ]
    fused = pl.pallas_call(
        functools.partial(fused_kernel, dims),
        out_shape=[pltpu.VMEM(shape, F32) for shape in kept],
        in_specs=[hbm] * 10,
        out_specs=[vmem] * len(kept),
        scratch_shapes=[
            pltpu.VMEM(board_shape, F32),
            pltpu.VMEM(board_shape, F32),
            pltpu.VMEM(history_mask.shape[::-1], jnp.int32),
            pltpu.VMEM((2, 2, chan), F32),
            pltpu.VMEM((2, 2, chan), F32),
            pltpu.VMEM((2, chan, kin), F32),
            pltpu.VMEM((2, chan, kin), BF16),
            pltpu.VMEM((span, chan), F32),
            pltpu.VMEM((rows + 2 * line, chunk), BF16),
            pltpu.VMEM((rows + 2 * line, chunk), BF16),
            pltpu.VMEM((rows + 2 * line, chunk), BF16),
            pltpu.VMEM((rows, chan), F32),
            pltpu.VMEM((rows, chan), F32),
            pltpu.VMEM((rows, chan), F32),
            pltpu.VMEM((rows, chan), F32),
            pltpu.VMEM((rows, chan), F32),
            pltpu.VMEM((2, kin, chan), F32),
            pltpu.VMEM((4, ndev, 2, chan), F32),
            pltpu.VMEM((2, 3, chunk // 2, chan), F32),
            pltpu.VMEM((2, 3, chunk // 4, chan), F32),
            pltpu.VMEM((2, 3, chunk // 8, chan), F32),
            pltpu.VMEM((2, 3, 3, chunk // 32, chan), F32),
            pltpu.VMEM((2, 3, max(extra, 1), chunk // 32, chan), F32),
            pltpu.SemaphoreType.DMA((25,)),
            pltpu.SemaphoreType.DMA((4,)),
            pltpu.SemaphoreType.DMA((4,)),
            pltpu.SemaphoreType.DMA((2, 3, 12 + extra)),
            pltpu.SemaphoreType.DMA((2, 3, 12 + extra)),
        ],
        compiler_params=pltpu.CompilerParams(
            collective_id=0, has_side_effects=True, vmem_limit_bytes=34 * MIB
        ),
        name="fused_passes",
    )
    held = fused(
        boards,
        history_mask.T,
        kernels,
        norm_params,
        norm_momenta,
        left_stats,
        left_roots,
        jnp.swapaxes(right_stats, 1, 2),
        jnp.swapaxes(right_roots, 1, 2),
        out_cotangent,
    )
    finish = pl.pallas_call(
        functools.partial(finish_kernel, dims),
        out_shape=[
            pltpu.HBM(boards.shape, F32),
            pltpu.HBM(boards.shape, F32),
            pltpu.HBM((2, share_width, chan), F32),
            pltpu.HBM((2, share_width, chan), F32),
            pltpu.HBM((2, chan, chan), F32),
            pltpu.HBM((2, share_width, kin), F32),
            pltpu.HBM((2, 2, chan), F32),
            pltpu.HBM((2, 2, chan), F32),
        ],
        in_specs=[vmem] * len(kept),
        out_specs=[hbm] * 8,
        scratch_shapes=[
            pltpu.VMEM((2, kin, chan), BF16),
            pltpu.VMEM((2, 3, share_width, chunk), F32),
            pltpu.VMEM((2, share_width, chan), F32),
            pltpu.VMEM((2, chan, chan), F32),
            pltpu.SemaphoreType.DMA((32,)),
        ],
        compiler_params=pltpu.CompilerParams(vmem_limit_bytes=24 * MIB),
        name="finish",
    )
    block_out, board_grad, grad, kernel, left, right, momenta, params = finish(*held)
    return (
        block_out,
        board_grad,
        jnp.swapaxes(grad, 1, 2),
        jnp.swapaxes(kernel, 1, 2),
        left,
        jnp.swapaxes(right, 1, 2),
        momenta,
        params,
    )


def solution(mesh):
    nw, nn = mesh.shape["wide"], mesh.shape["narrow"]
    boards = P(("wide", "narrow"), None, None, None)
    columns = P(None, None, "narrow")
    in_specs = (
        boards,
        P(("wide", "narrow"), None),
        P(),
        P(),
        P(),
        P(),
        columns,
        P(),
        columns,
        boards,
    )
    out_specs = (boards, boards, columns, columns, P(), columns, P(), P())
    return jax.shard_map(
        functools.partial(body, nw, nn),
        mesh=mesh,
        in_specs=in_specs,
        out_specs=out_specs,
        check_vma=False,
    )
```

```python
import functools
import math

import jax
import jax.numpy as jnp
from jax import lax
from jax.experimental import pallas as pl
from jax.experimental.pallas import tpu as pltpu
from jax.sharding import PartitionSpec as P

EPS = 1e-05
MOMENTUM = 0.9
NORM_RATE = 50.0
KERNEL_RATE = 0.1
STAT_DECAY = 0.5

SIDE = 8
CUBE = 0.044715
ROOT = math.sqrt(2.0 / math.pi)
MESH = pl.DeviceIdType.MESH
F32 = jnp.float32
BF16 = jnp.bfloat16
MIB = 2**20


PIECES = (
    (1, 1, "c12z"), (1, 1, "cz12"), (1, 1, "cz12"), (1, 2, "c12ab"),
    (1, 2, "c12ab"), (1, 1, "c12z"), (1, 1, "c12z"), (0, 1, "c1ab2"),
    (0, 2, "c12z"), (0, 1, "cab12"), (0, 1, "c12ab"), (0, 3, "c12z"),
    (0, 1, "c12z"),
)
ORDER = (
    3, -1, -1, -1, -2, 3, 6, 5, 2, 4, 6, 0, 5, 2, 1, 4, 1, 3, 0, -3,
    6, 9, 7, 10, 12, 5, 9, 7, 11, 4, 8, 3, 0, 10, 6, 12, 5, 2, 7, 11,
    9, 4, 0, 3, 10, 12, 7, 8, 5, -4, 4, 6, 11, 2, 10, 12, 3, 1, 0, 7,
    9, 8, 10, 5, 4, 11, 9, 6, 7, 3, 1, 2, 12, 5, 9, 0, 10, 4, 6, 7,
    1, 8, 3, 2, 9, 0, 11, -4, 12, 4, 10, 6, 3, 1, 9, 7, 8, 12, 10, 4,
    2, 0, 11, -4, 1, 7, 0, 10, 8, 9, 11, 4, 3, 4, 8, 9, 5, 2, 10, 9,
    12, 1, 10, 11, 3, 2, 7, 8, 5, 6, 1, 12, 11, -5, 7, 8,
)


def dot(lhs, rhs, lhs_dim, rhs_dim):
    return lax.dot_general(
        lhs, rhs, (((lhs_dim,), (rhs_dim,)), ((), ())), preferred_element_type=F32
    )


def gelu_tanh(v):
    return jnp.tanh(ROOT * (v + CUBE * (v * v * v)))


def gelu_slope(v, t):
    inner = ROOT * (1.0 + (3.0 * CUBE) * (v * v))
    return 0.5 * (1.0 + t) + (0.5 * v) * ((1.0 - t * t) * inner)


def flip(index, bit):
    return index + (1 - 2 * ((index // (1 << bit)) % 2)) * (1 << bit)


def bit_of(index, bit):
    return (index // (1 << bit)) % 2


def pick(taken, one, other):
    return taken * one + (1 - taken) * other


def fused_kernel(
    dims,
    boards,
    mask_t,
    kernels,
    params,
    momenta,
    left_stats,
    left_roots,
    right_stats,
    right_roots,
    cotangent,
    g_full,
    stats_v,
    roots_v,
    lstats_v,
    lroots_v,
    kt,
    bo,
    bg,
    new_momenta,
    new_params,
    bd,
    ct,
    mk,
    par,
    mom,
    kf,
    wb,
    ktmp,
    x_one,
    x_two,
    dgrid,
    h_one,
    slope_one,
    h_two,
    d_sum,
    d_hid,
    gp,
    red,
    arrived,
    load_sem,
    red_send,
    red_recv,
    g_send,
    g_recv,
):
    nw, nn, pos, chan = dims
    line = pos * SIDE
    rows = line * SIDE
    count = float(rows * nw * nn)
    chunk = 3 * chan
    wide, narrow = lax.axis_index("wide"), lax.axis_index("narrow")
    me = wide * nn + narrow
    extra_bits = list(range(3, nw.bit_length() - 1))

    def load(slot, src, dst):
        copy = pltpu.make_async_copy(src, dst, load_sem.at[slot])
        copy.start()
        return copy

    got_k0 = load(0, kernels.at[0], kf)
    got_mask = load(1, mask_t, mk)
    got_boards = [load(2 + i, boards.at[:, i], bd.at[i]) for i in range(SIDE)]
    got_par = load(10, params, par)

    def each_other(act):
        if nw * nn <= 32:
            for k in range(nw * nn - 1, 0, -1):
                w, n = wide, narrow
                for b in range(nw.bit_length() - 1):
                    if (k // nn) >> b & 1:
                        w = flip(w, b) if b == 0 else w + (flip(wide, b) - wide)
                for b in range(nn.bit_length() - 1):
                    if (k % nn) >> b & 1:
                        n = n + (flip(narrow, b) - narrow)
                act((w, n))
        else:

            @pl.loop(1, nw * nn)
            def _(k):
                other = lax.rem(me + k, nw * nn)
                act((other // nn, lax.rem(other, nn)))

    barrier = pltpu.get_barrier_semaphore()
    each_other(
        lambda dev: pl.semaphore_signal(barrier, inc=1, device_id=dev, device_id_type=MESH)
    )

    def share(slot, value):
        red[slot, me] = value

        def send(dev):
            pltpu.make_async_remote_copy(
                src_ref=red.at[slot, me],
                dst_ref=red.at[slot, me],
                send_sem=red_send.at[slot],
                recv_sem=red_recv.at[slot],
                device_id=dev,
                device_id_type=MESH,
            ).start()

        each_other(send)

    def collect(slot):
        others = red.at[slot, pl.ds(0, nw * nn - 1)]
        pltpu.make_async_copy(others, others, red_recv.at[slot]).wait()
        pltpu.make_async_copy(others, others, red_send.at[slot]).wait()
        return red[slot]

    def moments(slot):
        got = collect(slot)
        means, spreads = got[:, 0, :], got[:, 1, :]
        mean = jnp.sum(means, axis=0, keepdims=True) * (1.0 / (nw * nn))
        gap = means - mean
        spread = jnp.sum(spreads, axis=0, keepdims=True) + float(rows) * jnp.sum(
            gap * gap, axis=0, keepdims=True
        )
        return mean, lax.rsqrt(spread / count + EPS)

    def totals(slot):
        got = collect(slot)
        return (
            jnp.sum(got[:, 0, :], axis=0, keepdims=True),
            jnp.sum(got[:, 1, :], axis=0, keepdims=True),
        )

    def local_moments(ref):
        total = jnp.sum(ref[...], axis=0, keepdims=True)
        mean = total * (1.0 / rows)
        gap = ref[...] - mean
        return jnp.concatenate([mean, jnp.sum(gap * gap, axis=0, keepdims=True)], axis=0)

    column = lax.broadcasted_iota(jnp.int32, (pos, SIDE, chan), 1)

    def put_shifted(grid, i, value):
        cube = value.reshape(pos, SIDE, chan)
        before = jnp.where(column == 0, 0.0, pltpu.roll(cube, 1, 1))
        after = jnp.where(column == SIDE - 1, 0.0, pltpu.roll(cube, SIDE - 1, 1))
        at = pl.ds(pl.multiple_of((i + 1) * line, 16), line)
        grid[at, 0:chan] = before.reshape(line, chan).astype(BF16)
        grid[at, chan : 2 * chan] = value.astype(BF16)
        grid[at, 2 * chan : 3 * chan] = after.reshape(line, chan).astype(BF16)

    def at_line(i):
        return pl.ds(pl.multiple_of(i * line, 8), line)

    def conv(grid, k):
        return sum(
            dot(
                grid[a * line : a * line + rows, :],
                wb[k, :, a * chunk : (a + 1) * chunk],
                1,
                1,
            )
            for a in range(3)
        )

    def conv_back(grid, k, a):
        result = None
        for b in range(3):
            tap = 3 * (2 - a) + (2 - b)
            term = dot(
                grid[a * line : a * line + rows, b * chan : (b + 1) * chan],
                wb[k, :, tap * chan : (tap + 1) * chan],
                1,
                0,
            )
            result = term if result is None else result + term
        return result

    core = bit_of(narrow, 0)
    x_bit, y_bit = bit_of(narrow, 1), bit_of(wide, 0)
    z_low, z_high = bit_of(wide, 1), bit_of(wide, 2)
    z_pos = z_low + 2 * z_high
    x_dev = (wide, flip(narrow, 1))
    y_dev = (flip(wide, 0), narrow)
    pairs = {
        "c": ((wide, flip(narrow, 0)), core),
        "1": (
            (pick(core, y_dev[0], x_dev[0]), pick(core, y_dev[1], x_dev[1])),
            pick(core, y_bit, x_bit),
        ),
        "2": (
            (pick(core, x_dev[0], y_dev[0]), pick(core, x_dev[1], y_dev[1])),
            pick(core, x_bit, y_bit),
        ),
        "a": ((flip(wide, 1), narrow), z_low),
        "b": ((flip(wide, 2), narrow), z_high),
    }
    line_devs = []
    for q in (3, 2, 1):
        other = (1 - z_low if q & 1 else z_low) + 2 * (1 - z_high if q & 2 else z_high)
        line_devs.append((other, (wide + 2 * (other - z_pos), narrow)))

    sends, done = [], []
    filled = [0, 0]

    def remote(src, dst, dev):
        slot = len(sends)
        copy = pltpu.make_async_remote_copy(
            src_ref=src,
            dst_ref=dst,
            send_sem=g_send.at[slot],
            recv_sem=g_recv.at[slot],
            device_id=dev,
            device_id_type=MESH,
        )
        copy.start()
        sends.append(copy)
        return copy

    def at(start, size):
        return pl.ds(pl.multiple_of(start, 8), size)

    def take(k, size):
        start = filled[k]
        filled[k] += size
        return pl.ds(start, size)

    def piece(k, base, size, kind, compute):
        starts, sizes, live = [base], [size], {}
        for step in kind:
            place = z_pos if step == "z" else pairs[step][1]
            sizes.append(sizes[-1] // (4 if step == "z" else 2))
            starts.append(starts[-1] + place * sizes[-1])
        last = len(kind) - 1
        own = at(starts[-1], sizes[-1])

        def scatter(i):
            part = sizes[i + 1]
            if kind[i] == "z":
                targets = line_devs
            else:
                dev, place = pairs[kind[i]]
                targets = [(1 - place, dev)]
            live[i] = []
            for place, dev in targets:
                into = take(k, part)
                src = gp.at[k, at(starts[i] + place * part, part)]
                live[i].append((remote(src, arrived.at[k, into], dev), into))

        def add(i):
            rows_here = at(starts[i + 1], sizes[i + 1])
            value = gp[k, rows_here]
            for copy, into in live[i]:
                copy.wait_recv()
                value = value + arrived[k, into]
            return rows_here, value

        def gather(i):
            ref = g_full.at[k, at(starts[i + 1], sizes[i + 1])]
            targets = line_devs if kind[i] == "z" else [(0, pairs[kind[i]][0])]
            live[i] = [remote(ref, ref, dev) for _, dev in targets]

        def start():
            compute()
            scatter(0)

        def middle(i):
            rows_here, value = add(i)
            gp[k, rows_here] = value
            scatter(i + 1)

        def turn():
            _, value = add(last)
            for b in extra_bits:
                gp[k, own] = value
                into = take(k, sizes[-1])
                copy = remote(gp.at[k, own], arrived.at[k, into], (flip(wide, b), narrow))
                copy.wait()
                done.append(copy)
                value = value + arrived[k, into]
            g_full[k, own] = value * (1.0 / count)
            gather(last)

        def back(i):
            for copy in live[i]:
                copy.wait_recv()
            if i:
                gather(i - 1)

        return (
            [start]
            + [functools.partial(middle, i) for i in range(last)]
            + [turn]
            + [functools.partial(back, i) for i in range(last, -1, -1)]
        )

    empty = jnp.zeros((line, 3 * chan), BF16)
    for grid in (x_one, x_two, dgrid):
        grid[0:line, :] = empty
        grid[line + rows : 2 * line + rows, :] = empty

    got_mask.wait()
    hist = mk.shape[0]
    width = chan // hist
    spot = lax.broadcasted_iota(jnp.int32, (pos, line), 1)
    owner = SIDE * lax.broadcasted_iota(jnp.int32, (pos, line), 0)
    spread_pos = jnp.where((spot >= owner) & (spot < owner + SIDE), 1.0, 0.0).astype(BF16)
    spot = lax.broadcasted_iota(jnp.int32, (hist, chan), 1)
    owner = width * lax.broadcasted_iota(jnp.int32, (hist, chan), 0)
    spread_chan = jnp.where((spot >= owner) & (spot < owner + width), 1.0, 0.0).astype(BF16)
    by_row = dot(mk[...].astype(F32).astype(BF16), spread_pos, 1, 0).astype(BF16)
    planes = dot(by_row, spread_chan, 0, 0)

    got_k0.wait()
    wb[0] = kf[...].astype(BF16)
    got_ct = [load(12 + i, cotangent.at[:, i], ct.at[i]) for i in range(SIDE)]
    for i in range(SIDE):
        got_boards[i].wait()
        value = bd[i].reshape(line, chan) * planes
        bd[i] = value.reshape(pos, SIDE, chan)
        put_shifted(x_one, i, value)

    h_one[...] = conv(x_one, 0)
    local = local_moments(h_one)
    pl.semaphore_wait(barrier, nw * nn - 1)
    share(0, local)

    got_par.wait()

    def keep_share(k):
        share_width = kt.shape[1]
        span = ktmp.shape[0]
        start = narrow * share_width
        block = (start // 128) * 128
        ktmp[...] = kf[:, pl.ds(pl.multiple_of(block, 128), span)].T
        kt[k] = ktmp[pl.ds(pl.multiple_of(start - block, 8), share_width), :]

    keep_share(0)
    got_k1 = load(11, kernels.at[1], kf)
    late = [
        load(20, momenta, mom),
        load(21, left_stats, lstats_v),
        load(22, left_roots, lroots_v),
        load(23, right_roots, roots_v),
        load(24, right_stats, stats_v),
    ]
    got_k1.wait()
    wb[1] = kf[...].astype(BF16)
    keep_share(1)

    gain_one, shift_one = par[0, 0:1, :], par[0, 1:2, :]
    gain_two, shift_two = par[1, 0:1, :], par[1, 1:2, :]

    mean_one, inv_one = moments(0)

    @pl.loop(0, SIDE)
    def _(i):
        at = at_line(i)
        normed = (h_one[at, :] - mean_one) * inv_one
        h_one[at, :] = normed
        pre = normed * gain_one + shift_one
        put_shifted(x_two, i, (0.5 * pre) * (1.0 + gelu_tanh(pre)))

    h_two[...] = conv(x_two, 1)
    share(1, local_moments(h_two))

    @pl.loop(0, SIDE)
    def _(i):
        at = at_line(i)
        pre = h_one[at, :] * gain_one + shift_one
        slope_one[at, :] = gelu_slope(pre, gelu_tanh(pre))

    for copy in got_ct:
        copy.wait()
    mean_two, inv_two = moments(1)

    def fold(value):
        return jnp.sum(value.reshape(pos, SIDE, chan), axis=0)

    nothing = jnp.zeros((SIDE, chan), F32)

    def close(gain_sum, shift_sum):
        return jnp.concatenate(
            [
                jnp.sum(gain_sum, axis=0, keepdims=True),
                jnp.sum(shift_sum, axis=0, keepdims=True),
            ],
            axis=0,
        )

    def out_line(i, carry):
        at = at_line(i)
        normed = (h_two[at, :] - mean_two) * inv_two
        h_two[at, :] = normed
        summed = bd[i].reshape(line, chan) + normed * gain_two + shift_two
        t = gelu_tanh(summed)
        bo[i] = ((0.5 * summed) * (1.0 + t)).reshape(pos, SIDE, chan)
        slope = ct[i].reshape(line, chan) * gelu_slope(summed, t)
        d_sum[at, :] = slope
        return carry[0] + fold(slope * normed), carry[1] + fold(slope)

    share(2, close(*lax.fori_loop(0, SIDE, out_line, (nothing, nothing))))

    gain_two_sum, shift_two_sum = totals(2)
    scale_two = gain_two * inv_two

    @pl.loop(0, SIDE)
    def _(i):
        at = at_line(i)
        lost = (shift_two_sum + h_two[at, :] * gain_two_sum) * (1.0 / count)
        put_shifted(dgrid, i, scale_two * (d_sum[at, :] - lost))

    def weights(k, first, taps_here):
        grid = (x_one, x_two)[k]
        tap = first
        while tap < first + taps_here:
            a, b = divmod(tap, 3)
            n = min(3 - b, first + taps_here - tap)
            g_part = dot(
                grid[a * line : a * line + rows, b * chan : (b + n) * chan],
                dgrid[line : line + rows, chan : 2 * chan],
                0,
                0,
            )
            gp[k, tap * chan : (tap + n) * chan, :] = g_part
            tap += n

    def add_back(k, a):
        term = conv_back(dgrid, k, a)
        d_hid[...] = d_hid[...] + term if a else term

    kept = {}

    def pre_sums():
        def pre_line(i, carry):
            at = at_line(i)
            d_pre = d_hid[at, :] * slope_one[at, :]
            d_hid[at, :] = d_pre
            return carry[0] + fold(d_pre * h_one[at, :]), carry[1] + fold(d_pre)

        share(3, close(*lax.fori_loop(0, SIDE, pre_line, (nothing, nothing))))

    def first_conv_grad():
        kept["sums"] = gain_one_sum, shift_one_sum = totals(3)
        scale_one = gain_one * inv_one

        @pl.loop(0, SIDE)
        def _(i):
            at = at_line(i)
            lost = (shift_one_sum + h_one[at, :] * gain_one_sum) * (1.0 / count)
            put_shifted(dgrid, i, scale_one * (d_hid[at, :] - lost))

    def board_grads():
        for i in range(SIDE):
            at = at_line(i)
            bg[i] = ((d_sum[at, :] + d_hid[at, :]) * planes).reshape(pos, SIDE, chan)

    steps = []
    tap_at = [0, 0]
    for k, n, kind in PIECES:
        compute = functools.partial(weights, k, tap_at[k], n)
        steps.append(iter(piece(k, tap_at[k] * chan, n * chan, kind, compute)))
        tap_at[k] += n
    passes = {
        -1: iter([functools.partial(add_back, 1, a) for a in range(3)]),
        -2: iter([pre_sums]),
        -3: iter([first_conv_grad]),
        -4: iter([functools.partial(add_back, 0, a) for a in range(3)]),
        -5: iter([board_grads]),
    }
    for item in ORDER:
        next(steps[item] if item >= 0 else passes[item])()
    gain_one_sum, shift_one_sum = kept["sums"]

    for copy in late:
        copy.wait()
    norm_grad = [
        jnp.concatenate([gain_one_sum, shift_one_sum], axis=0),
        jnp.concatenate([gain_two_sum, shift_two_sum], axis=0),
    ]
    for k in range(2):
        value = MOMENTUM * mom[k] + norm_grad[k] * (1.0 / count)
        new_momenta[k] = value
        new_params[k] = par[k] - NORM_RATE * value

    for copy in sends:
        if not any(copy is other for other in done):
            copy.wait_send()


def finish_kernel(
    dims,
    g_full,
    stats,
    roots,
    lstats,
    lroots,
    kt,
    bo,
    bg,
    momenta,
    params,
    o_block,
    o_board,
    o_grad,
    o_kernel,
    o_left,
    o_right,
    o_momenta,
    o_params,
    gb,
    nr,
    nk,
    nl,
    sem,
):
    chan = dims[3]
    chunk = 3 * chan
    share_width = kt.shape[1]
    start = pl.multiple_of(lax.axis_index("narrow") * share_width, 8)
    copies = []

    def put(src, dst):
        copy = pltpu.make_async_copy(src, dst, sem.at[len(copies)])
        copy.start()
        copies.append(copy)

    for k in range(2):
        put(g_full.at[k, pl.ds(start, share_width)], o_grad.at[k])
        gb[k] = g_full[k].astype(BF16)
        own = g_full[k, pl.ds(start, share_width), :].astype(BF16)
        for q in range(3):
            cols = pl.ds(q * chunk, chunk)
            term = dot(own, gb[k, cols, :], 1, 1)
            nr[k, q] = STAT_DECAY * stats[k, :, cols] + (1.0 - STAT_DECAY) * term
            put(nr.at[k, q], o_right.at[k, :, cols])
        if k == 0:
            for i in range(SIDE):
                put(bo.at[i], o_block.at[:, i])
                put(bg.at[i], o_board.at[:, i])
            put(momenta, o_momenta)
            put(params, o_params)
    for k in range(2):
        term = dot(gb[k], gb[k], 0, 0)
        nl[k] = STAT_DECAY * lstats[k] + (1.0 - STAT_DECAY) * term
        put(nl.at[k], o_left.at[k])
        mixed = dot(roots[k].astype(BF16), gb[k], 1, 0)
        update = dot(mixed.astype(BF16), lroots[k].astype(BF16), 1, 1)
        nk[k] = kt[k] - KERNEL_RATE * update
        put(nk.at[k], o_kernel.at[k])
    for copy in copies:
        copy.wait()


def room_of(size, kind, extra):
    rows = 0
    for step in kind:
        size //= 4 if step == "z" else 2
        rows += 3 * size if step == "z" else size
    return rows + extra * size


def body(
    nw,
    nn,
    boards,
    history_mask,
    kernels,
    norm_params,
    norm_momenta,
    left_stats,
    right_stats,
    left_roots,
    right_roots,
    out_cotangent,
):
    pos, chan = boards.shape[0], boards.shape[3]
    kin = kernels.shape[2]
    share_width = right_stats.shape[2]
    line = pos * SIDE
    rows = line * SIDE
    chunk = 3 * chan
    ndev = nw * nn
    extra = max(nw.bit_length() - 4, 0)
    dims = (nw, nn, pos, chan)
    hbm = pl.BlockSpec(memory_space=pl.ANY)
    vmem = pl.BlockSpec(memory_space=pltpu.VMEM)
    span = -(-(share_width + 64) // 128) * 128
    board_shape = (SIDE, pos, SIDE, chan)

    kept = [
        (2, kin, chan),
        (2, share_width, kin),
        (2, share_width, kin),
        (2, chan, chan),
        (2, chan, chan),
        (2, share_width, chan),
        board_shape,
        board_shape,
        (2, 2, chan),
        (2, 2, chan),
    ]
    arrivals = max(
        sum(room_of(n * chan, kind, extra) for layer, n, kind in PIECES if layer == k)
        for k in range(2)
    )
    transfers = sum(2 * len(kind) + 4 * kind.count("z") + extra for _, _, kind in PIECES)
    room = (49 + extra) * MIB // 2 + (ndev - 32) * 8 * chan * 4 + 8 * chan * max(arrivals - kin, 0)
    fused = pl.pallas_call(
        functools.partial(fused_kernel, dims),
        out_shape=[pltpu.VMEM(shape, F32) for shape in kept],
        in_specs=[hbm] * 10,
        out_specs=[vmem] * len(kept),
        scratch_shapes=[
            pltpu.VMEM(board_shape, F32),
            pltpu.VMEM(board_shape, F32),
            pltpu.VMEM(history_mask.shape[::-1], jnp.int32),
            pltpu.VMEM((2, 2, chan), F32),
            pltpu.VMEM((2, 2, chan), F32),
            pltpu.VMEM((chan, kin), F32),
            pltpu.VMEM((2, chan, kin), BF16),
            pltpu.VMEM((span, chan), F32),
            pltpu.VMEM((rows + 2 * line, chunk), BF16),
            pltpu.VMEM((rows + 2 * line, chunk), BF16),
            pltpu.VMEM((rows + 2 * line, chunk), BF16),
            pltpu.VMEM((rows, chan), F32),
            pltpu.VMEM((rows, chan), F32),
            pltpu.VMEM((rows, chan), F32),
            pltpu.VMEM((rows, chan), F32),
            pltpu.VMEM((rows, chan), F32),
            pltpu.VMEM((2, kin, chan), F32),
            pltpu.VMEM((4, ndev, 2, chan), F32),
            pltpu.VMEM((2, arrivals, chan), F32),
            pltpu.SemaphoreType.DMA((25,)),
            pltpu.SemaphoreType.DMA((4,)),
            pltpu.SemaphoreType.DMA((4,)),
            pltpu.SemaphoreType.DMA((transfers,)),
            pltpu.SemaphoreType.DMA((transfers,)),
        ],
        compiler_params=pltpu.CompilerParams(
            collective_id=0, has_side_effects=True, vmem_limit_bytes=room
        ),
        name="fused_passes",
    )
    given = (
        boards,
        history_mask.T,
        kernels,
        norm_params,
        norm_momenta,
        left_stats,
        left_roots,
        jnp.swapaxes(right_stats, 1, 2),
        jnp.swapaxes(right_roots, 1, 2),
        out_cotangent,
    )
    held = fused(*(pltpu.with_memory_space_constraint(v, pltpu.HBM) for v in given))
    held = [pltpu.with_memory_space_constraint(v, pltpu.VMEM) for v in held]
    finish = pl.pallas_call(
        functools.partial(finish_kernel, dims),
        out_shape=[
            pltpu.HBM(boards.shape, F32),
            pltpu.HBM(boards.shape, F32),
            pltpu.HBM((2, share_width, chan), F32),
            pltpu.HBM((2, share_width, chan), F32),
            pltpu.HBM((2, chan, chan), F32),
            pltpu.HBM((2, share_width, kin), F32),
            pltpu.HBM((2, 2, chan), F32),
            pltpu.HBM((2, 2, chan), F32),
        ],
        in_specs=[vmem] * len(kept),
        out_specs=[hbm] * 8,
        scratch_shapes=[
            pltpu.VMEM((2, kin, chan), BF16),
            pltpu.VMEM((2, 3, share_width, chunk), F32),
            pltpu.VMEM((2, share_width, chan), F32),
            pltpu.VMEM((2, chan, chan), F32),
            pltpu.SemaphoreType.DMA((32,)),
        ],
        compiler_params=pltpu.CompilerParams(vmem_limit_bytes=20 * MIB),
        name="finish",
    )
    block_out, board_grad, grad, kernel, left, right, momenta, params = finish(*held)
    return (
        block_out,
        board_grad,
        jnp.swapaxes(grad, 1, 2),
        jnp.swapaxes(kernel, 1, 2),
        left,
        jnp.swapaxes(right, 1, 2),
        momenta,
        params,
    )


def solution(mesh):
    nw, nn = mesh.shape["wide"], mesh.shape["narrow"]
    boards = P(("wide", "narrow"), None, None, None)
    columns = P(None, None, "narrow")
    in_specs = (
        boards,
        P(("wide", "narrow"), None),
        P(),
        P(),
        P(),
        P(),
        columns,
        P(),
        columns,
        boards,
    )
    out_specs = (boards, boards, columns, columns, P(), columns, P(), P())
    return jax.shard_map(
        functools.partial(body, nw, nn),
        mesh=mesh,
        in_specs=in_specs,
        out_specs=out_specs,
        check_vma=False,
    )
```

```python
import functools
import math

import jax
import jax.numpy as jnp
from jax import lax
from jax.experimental import pallas as pl
from jax.experimental.pallas import tpu as pltpu
from jax.sharding import PartitionSpec as P

EPS = 1e-05
MOMENTUM = 0.9
NORM_RATE = 50.0
KERNEL_RATE = 0.1
STAT_DECAY = 0.5

SIDE = 8
CUBE = 0.044715
ROOT = math.sqrt(2.0 / math.pi)
MESH = pl.DeviceIdType.MESH
F32 = jnp.float32
BF16 = jnp.bfloat16
MIB = 2**20


PIECES = (
    (1, 1, "c12z"), (1, 1, "cz12"), (1, 1, "c12ab"), (1, 1, "cab12"),
    (1, 1, "c12ab"), (1, 2, "c12z"), (1, 1, "c12ab"), (1, 1, "c12z"),
    (0, 1, "c12ab"), (0, 1, "c12z"), (0, 1, "c12z"), (0, 1, "c12ab"),
    (0, 1, "c12z"), (0, 2, "c12ab"), (0, 1, "c12z"), (0, 1, "cab12"),
)
ORDER = (
    2, 6, 5, -1, 3, 2, -1, 6, -1, -2, 3, 5, 7, 1, 0, 4, 7, 4, 2, 1,
    6, 3, 5, 0, -3, 8, 15, 13, 7, 2, 4, 6, 8, 15, 12, 10, 13, 5, 0, -4,
    1, 12, 7, 11, 2, 9, 3, 4, 6, 8, 14, 11, 10, 15, 13, 0, 12, 9, 1, 4,
    8, 2, 6, 3, 7, 11, 5, 14, 10, 13, 15, 12, 9, 4, 8, 11, 3, 2, 6, 0,
    1, 14, 10, 15, 13, 7, 9, 5, -4, 1, 8, 4, 11, 12, 2, 15, 3, 6, 7, 14,
    0, 13, 10, 5, -4, 4, 8, 9, 11, 15, 3, 2, 12, 0, -5, 13, 6, 14, 8, 15,
    5, 4, 11, 10, 12, 7, 1, 9, 3, 13, 8, 14, 11, 0, 10, 2, 15, 4, 9, 12,
    6, 13, 12, 7, 14, 6, 8, 11, 0, 3, 5, 1, 10, 9, 8, 3, 2, 4, 15, 1,
    -7, -7, 13, 14, -7, 11, -7, 10, 15, 14, 9, 13, 11,
)


def dot(lhs, rhs, lhs_dim, rhs_dim):
    return lax.dot_general(
        lhs, rhs, (((lhs_dim,), (rhs_dim,)), ((), ())), preferred_element_type=F32
    )


def gelu_tanh(v):
    return jnp.tanh(ROOT * (v + CUBE * (v * v * v)))


def gelu_slope(v, t):
    inner = ROOT * (1.0 + (3.0 * CUBE) * (v * v))
    return 0.5 * (1.0 + t) + (0.5 * v) * ((1.0 - t * t) * inner)


def flip(index, bit):
    return index + (1 - 2 * ((index // (1 << bit)) % 2)) * (1 << bit)


def bit_of(index, bit):
    return (index // (1 << bit)) % 2


def pick(taken, one, other):
    return taken * one + (1 - taken) * other


def fused_kernel(
    dims,
    boards,
    mask_t,
    kernels,
    params,
    momenta,
    left_stats,
    left_roots,
    right_stats,
    right_roots,
    cotangent,
    g_full,
    stats_v,
    roots_v,
    lstats_v,
    lroots_v,
    kt,
    bo,
    bg,
    new_momenta,
    new_params,
    bd,
    ct,
    mk,
    par,
    mom,
    kf,
    wb,
    x_one,
    x_two,
    dgrid,
    h_one,
    slope_one,
    h_two,
    d_sum,
    d_hid,
    gp,
    red,
    arrived,
    load_sem,
    red_send,
    red_recv,
    g_send,
    g_recv,
):
    nw, nn, pos, chan = dims
    line = pos * SIDE
    rows = line * SIDE
    count = float(rows * nw * nn)
    chunk = 3 * chan
    wide, narrow = lax.axis_index("wide"), lax.axis_index("narrow")
    me = wide * nn + narrow
    extra_bits = list(range(3, nw.bit_length() - 1))

    def load(slot, src, dst):
        copy = pltpu.make_async_copy(src, dst, load_sem.at[slot])
        copy.start()
        return copy

    got_mask = load(0, mask_t, mk)
    for i in range(SIDE):
        load(1, boards.at[:, i], bd.at[i])
    got_k0 = [
        load(9 + a, kernels.at[0, :, pl.ds(a * chunk, chunk)], kf.at[:, pl.ds(a * chunk, chunk)])
        for a in range(3)
    ]
    got_par = load(3, params, par)

    def each_other(act):
        if nw * nn <= 32:
            for k in range(nw * nn - 1, 0, -1):
                w, n = wide, narrow
                for b in range(nw.bit_length() - 1):
                    if (k // nn) >> b & 1:
                        w = flip(w, b) if b == 0 else w + (flip(wide, b) - wide)
                for b in range(nn.bit_length() - 1):
                    if (k % nn) >> b & 1:
                        n = n + (flip(narrow, b) - narrow)
                act((w, n))
        else:

            @pl.loop(1, nw * nn)
            def _(k):
                other = lax.rem(me + k, nw * nn)
                act((other // nn, lax.rem(other, nn)))

    barrier = pltpu.get_barrier_semaphore()
    each_other(
        lambda dev: pl.semaphore_signal(barrier, inc=1, device_id=dev, device_id_type=MESH)
    )

    def share(slot, value):
        red[slot, me] = value

        def send(dev):
            pltpu.make_async_remote_copy(
                src_ref=red.at[slot, me],
                dst_ref=red.at[slot, me],
                send_sem=red_send.at[0],
                recv_sem=red_recv.at[slot % 2],
                device_id=dev,
                device_id_type=MESH,
            ).start()

        each_other(send)

    def collect(slot):
        others = red.at[slot, pl.ds(0, nw * nn - 1)]
        pltpu.make_async_copy(others, others, red_recv.at[slot % 2]).wait()
        pltpu.make_async_copy(others, others, red_send.at[0]).wait()
        return red[slot]

    def moments(slot):
        got = collect(slot)
        means, spreads = got[:, 0, :], got[:, 1, :]
        mean = jnp.sum(means, axis=0, keepdims=True) * (1.0 / (nw * nn))
        gap = means - mean
        spread = jnp.sum(spreads, axis=0, keepdims=True) + float(rows) * jnp.sum(
            gap * gap, axis=0, keepdims=True
        )
        return mean, lax.rsqrt(spread / count + EPS)

    def totals(slot):
        got = collect(slot)
        return (
            jnp.sum(got[:, 0, :], axis=0, keepdims=True),
            jnp.sum(got[:, 1, :], axis=0, keepdims=True),
        )

    def local_moments(ref):
        total = jnp.sum(ref[...], axis=0, keepdims=True)
        mean = total * (1.0 / rows)
        gap = ref[...] - mean
        return jnp.concatenate([mean, jnp.sum(gap * gap, axis=0, keepdims=True)], axis=0)

    column = lax.broadcasted_iota(jnp.int32, (pos, SIDE, chan), 1)

    def put_shifted(grid, i, value):
        cube = value.reshape(pos, SIDE, chan)
        before = jnp.where(column == 0, 0.0, pltpu.roll(cube, 1, 1))
        after = jnp.where(column == SIDE - 1, 0.0, pltpu.roll(cube, SIDE - 1, 1))
        at = pl.ds(pl.multiple_of((i + 1) * line, 16), line)
        grid[at, 0:chan] = before.reshape(line, chan).astype(BF16)
        grid[at, chan : 2 * chan] = value.astype(BF16)
        grid[at, 2 * chan : 3 * chan] = after.reshape(line, chan).astype(BF16)

    def at_line(i):
        return pl.ds(pl.multiple_of(i * line, 8), line)

    def conv(grid, k, result):
        tile = rows // 2

        @pl.loop(0, 2)
        def _(i):
            result[pl.ds(pl.multiple_of(i * tile, 8), tile), :] = sum(
                dot(
                    grid[pl.ds(pl.multiple_of(a * line + i * tile, 16), tile), :],
                    wb[k, :, a * chunk : (a + 1) * chunk],
                    1,
                    1,
                )
                for a in range(3)
            )

    def conv_back(grid, k, a):
        result = None
        for b in range(3):
            tap = 3 * (2 - a) + (2 - b)
            term = dot(
                grid[a * line : a * line + rows, b * chan : (b + 1) * chan],
                wb[k, :, tap * chan : (tap + 1) * chan],
                1,
                0,
            )
            result = term if result is None else result + term
        return result

    core = bit_of(narrow, 0)
    x_bit, y_bit = bit_of(narrow, 1), bit_of(wide, 0)
    z_low, z_high = bit_of(wide, 1), bit_of(wide, 2)
    z_pos = z_low + 2 * z_high
    x_dev = (wide, flip(narrow, 1))
    y_dev = (flip(wide, 0), narrow)
    pairs = {
        "c": ((wide, flip(narrow, 0)), core),
        "1": (
            (pick(core, y_dev[0], x_dev[0]), pick(core, y_dev[1], x_dev[1])),
            pick(core, y_bit, x_bit),
        ),
        "2": (
            (pick(core, x_dev[0], y_dev[0]), pick(core, x_dev[1], y_dev[1])),
            pick(core, x_bit, y_bit),
        ),
        "a": ((flip(wide, 1), narrow), z_low),
        "b": ((flip(wide, 2), narrow), z_high),
    }
    line_devs = []
    for q in (3, 2, 1):
        other = (1 - z_low if q & 1 else z_low) + 2 * (1 - z_high if q & 2 else z_high)
        line_devs.append((other, (wide + 2 * (other - z_pos), narrow)))

    filled = [0, 0]
    flags = iter(range(g_recv.shape[0]))
    sent = []

    def remote(src, dst, dev, send_sem, recv_sem):
        pltpu.make_async_remote_copy(
            src_ref=src,
            dst_ref=dst,
            send_sem=send_sem,
            recv_sem=recv_sem,
            device_id=dev,
            device_id_type=MESH,
        ).start()

    def wait_for(ref, sem):
        pltpu.make_async_copy(ref, ref, sem).wait()

    def at(start, size):
        return pl.ds(pl.multiple_of(start, 8), size)

    def piece(k, base, size, kind, compute):
        starts, sizes, into = [base], [size], []
        for step in kind:
            place = z_pos if step == "z" else pairs[step][1]
            sizes.append(sizes[-1] // (4 if step == "z" else 2))
            starts.append(starts[-1] + place * sizes[-1])
        last = len(kind) - 1
        own = at(starts[-1], sizes[-1])
        flag = [g_recv.at[next(flags)] for _ in kind]
        back_flag = [g_recv.at[next(flags)]] + flag[:-1]
        out_flag = g_send.at[len(sent)]
        sent.append((k, 2 * (size - sizes[-1]), out_flag))

        def scatter(i):
            part = sizes[i + 1]
            if kind[i] == "z":
                targets = line_devs
            else:
                dev, place = pairs[kind[i]]
                targets = [(1 - place, dev)]
            start = filled[k]
            into.append((start, part * len(targets)))
            filled[k] += part * len(targets)
            for q, (place, dev) in enumerate(targets):
                src = gp.at[k, at(starts[i] + place * part, part)]
                dst = arrived.at[k, pl.ds(start + q * part, part)]
                remote(src, dst, dev, out_flag, flag[i])

        def add(i):
            part = sizes[i + 1]
            start, total = into[i]
            wait_for(arrived.at[k, pl.ds(start, total)], flag[i])
            rows_here = at(starts[i + 1], part)
            value = gp[k, rows_here]
            for q in range(total // part):
                value = value + arrived[k, start + q * part : start + (q + 1) * part]
            return rows_here, value

        def gather(i):
            ref = g_full.at[k, at(starts[i + 1], sizes[i + 1])]
            targets = line_devs if kind[i] == "z" else [(0, pairs[kind[i]][0])]
            for _, dev in targets:
                remote(ref, ref, dev, out_flag, back_flag[i])

        def start():
            compute()
            scatter(0)

        def middle(i):
            rows_here, value = add(i)
            gp[k, rows_here] = value
            scatter(i + 1)

        def turn():
            _, value = add(last)
            for b in extra_bits:
                gp[k, own] = value
                into_more = arrived.at[k, pl.ds(filled[k], sizes[-1])]
                more = g_recv.at[next(flags)], g_recv.at[next(flags)]
                remote(gp.at[k, own], into_more, (flip(wide, b), narrow), *more)
                wait_for(into_more, more[0])
                wait_for(into_more, more[1])
                value = value + arrived[k, filled[k] : filled[k] + sizes[-1]]
                filled[k] += sizes[-1]
            g_full[k, own] = value * (1.0 / count)
            gather(last)

        def back(i):
            got = (3 if kind[i] == "z" else 1) * sizes[i + 1]
            wait_for(g_full.at[k, pl.ds(base, got)], back_flag[i])
            if i:
                gather(i - 1)

        return (
            [start]
            + [functools.partial(middle, i) for i in range(last)]
            + [turn]
            + [functools.partial(back, i) for i in range(last, -1, -1)]
        )

    def clear_ends(grid):
        empty = jnp.zeros((line, 3 * chan), BF16)
        grid[0:line, :] = empty
        grid[line + rows : 2 * line + rows, :] = empty

    clear_ends(x_one)
    got_mask.wait()
    hist = mk.shape[0]
    width = chan // hist
    spot = lax.broadcasted_iota(jnp.int32, (pos, line), 1)
    owner = SIDE * lax.broadcasted_iota(jnp.int32, (pos, line), 0)
    spread_pos = jnp.where((spot >= owner) & (spot < owner + SIDE), 1.0, 0.0).astype(BF16)
    spot = lax.broadcasted_iota(jnp.int32, (hist, chan), 1)
    owner = width * lax.broadcasted_iota(jnp.int32, (hist, chan), 0)
    spread_chan = jnp.where((spot >= owner) & (spot < owner + width), 1.0, 0.0).astype(BF16)
    by_row = dot(mk[...].astype(F32).astype(BF16), spread_pos, 1, 0).astype(BF16)
    planes = dot(by_row, spread_chan, 0, 0)

    pltpu.make_async_copy(bd, bd, load_sem.at[1]).wait()
    for i in range(SIDE):
        value = bd[i].reshape(line, chan) * planes
        bd[i] = value.reshape(pos, SIDE, chan)
        put_shifted(x_one, i, value)

    for a in range(3):
        got_k0[a].wait()
        part = slice(a * chunk, (a + 1) * chunk)
        wb[0, :, part] = kf[:, part].astype(BF16)
    conv(x_one, 0, h_one)
    local = local_moments(h_one)
    pl.semaphore_wait(barrier, nw * nn - 1)
    share(0, local)

    got_par.wait()

    def keep_share(k):
        share_width = kt.shape[1]
        span = -(-(share_width + 64) // 128) * 128
        start = narrow * share_width
        block = (start // 128) * 128
        d_hid[0:span, :] = kf[:, pl.ds(pl.multiple_of(block, 128), span)].T
        kt[k] = d_hid[pl.ds(pl.multiple_of(start - block, 8), share_width), :]

    clear_ends(x_two)
    clear_ends(dgrid)
    keep_share(0)
    got_k1 = load(4, kernels.at[1], kf)
    for i in range(SIDE):
        load(5, cotangent.at[:, i], ct.at[i])
    late = [
        load(6, momenta, mom),
        load(7, left_stats, lstats_v),
        load(8, left_roots, lroots_v),
        load(12, right_roots, roots_v),
        load(2, right_stats, stats_v),
    ]
    got_k1.wait()
    wb[1] = kf[...].astype(BF16)
    keep_share(1)

    gain_one, shift_one = par[0, 0:1, :], par[0, 1:2, :]
    gain_two, shift_two = par[1, 0:1, :], par[1, 1:2, :]

    mean_one, inv_one = moments(0)

    @pl.loop(0, SIDE)
    def _(i):
        at = at_line(i)
        normed = (h_one[at, :] - mean_one) * inv_one
        h_one[at, :] = normed
        pre = normed * gain_one + shift_one
        put_shifted(x_two, i, (0.5 * pre) * (1.0 + gelu_tanh(pre)))

    conv(x_two, 1, h_two)
    share(1, local_moments(h_two))

    @pl.loop(0, SIDE)
    def _(i):
        at = at_line(i)
        pre = h_one[at, :] * gain_one + shift_one
        slope_one[at, :] = gelu_slope(pre, gelu_tanh(pre))

    pltpu.make_async_copy(ct, ct, load_sem.at[5]).wait()
    mean_two, inv_two = moments(1)

    def fold(value):
        return jnp.sum(value.reshape(pos, SIDE, chan), axis=0)

    nothing = jnp.zeros((SIDE, chan), F32)

    def close(gain_sum, shift_sum):
        return jnp.concatenate(
            [
                jnp.sum(gain_sum, axis=0, keepdims=True),
                jnp.sum(shift_sum, axis=0, keepdims=True),
            ],
            axis=0,
        )

    def out_line(i, carry):
        at = at_line(i)
        normed = (h_two[at, :] - mean_two) * inv_two
        h_two[at, :] = normed
        summed = bd[i].reshape(line, chan) + normed * gain_two + shift_two
        t = gelu_tanh(summed)
        bo[i] = ((0.5 * summed) * (1.0 + t)).reshape(pos, SIDE, chan)
        slope = ct[i].reshape(line, chan) * gelu_slope(summed, t)
        d_sum[at, :] = slope
        return carry[0] + fold(slope * normed), carry[1] + fold(slope)

    share(2, close(*lax.fori_loop(0, SIDE, out_line, (nothing, nothing))))

    gain_two_sum, shift_two_sum = totals(2)
    scale_two = gain_two * inv_two

    @pl.loop(0, SIDE)
    def _(i):
        at = at_line(i)
        lost = (shift_two_sum + h_two[at, :] * gain_two_sum) * (1.0 / count)
        put_shifted(dgrid, i, scale_two * (d_sum[at, :] - lost))

    def weights(k, first, taps_here):
        grid = (x_one, x_two)[k]
        tap = first
        while tap < first + taps_here:
            a, b = divmod(tap, 3)
            n = min(3 - b, first + taps_here - tap)
            g_part = dot(
                grid[a * line : a * line + rows, b * chan : (b + n) * chan],
                dgrid[line : line + rows, chan : 2 * chan],
                0,
                0,
            )
            gp[k, tap * chan : (tap + n) * chan, :] = g_part
            tap += n

    def add_back(k, a):
        term = conv_back(dgrid, k, a)
        d_hid[...] = d_hid[...] + term if a else term

    kept = {}

    def pre_sums():
        def pre_line(i, carry):
            at = at_line(i)
            d_pre = d_hid[at, :] * slope_one[at, :]
            d_hid[at, :] = d_pre
            return carry[0] + fold(d_pre * h_one[at, :]), carry[1] + fold(d_pre)

        share(3, close(*lax.fori_loop(0, SIDE, pre_line, (nothing, nothing))))

    def first_conv_grad():
        kept["sums"] = gain_one_sum, shift_one_sum = totals(3)
        scale_one = gain_one * inv_one

        @pl.loop(0, SIDE)
        def _(i):
            at = at_line(i)
            lost = (shift_one_sum + h_one[at, :] * gain_one_sum) * (1.0 / count)
            put_shifted(dgrid, i, scale_one * (d_hid[at, :] - lost))

    def board_grads():
        for i in range(SIDE):
            at = at_line(i)
            bg[i] = ((d_sum[at, :] + d_hid[at, :]) * planes).reshape(pos, SIDE, chan)

    def second_left():
        for copy in late:
            copy.wait()
        for a in range(3):
            x_two[0:chunk, a * chan : (a + 1) * chan] = g_full[
                1, a * chunk : (a + 1) * chunk, :
            ].astype(BF16)
        blocks = [x_two[0:chunk, a * chan : (a + 1) * chan] for a in range(3)]
        term = sum(dot(block, block, 0, 0) for block in blocks)
        lstats_v[1] = STAT_DECAY * lstats_v[1] + (1.0 - STAT_DECAY) * term

    def second_right(a):
        width = kt.shape[1]
        start = pl.multiple_of(narrow * width, 8)
        own = g_full[1, pl.ds(start, width), :].astype(BF16)
        cols = slice(a * chunk, (a + 1) * chunk)
        term = dot(own, x_two[0:chunk, a * chan : (a + 1) * chan], 1, 1)
        stats_v[1, :, cols] = STAT_DECAY * stats_v[1, :, cols] + (1.0 - STAT_DECAY) * term

    def second_kernel():
        mixed = sum(
            dot(
                roots_v[1, :, a * chunk : (a + 1) * chunk].astype(BF16),
                x_two[0:chunk, a * chan : (a + 1) * chan],
                1,
                0,
            )
            for a in range(3)
        )
        update = dot(mixed.astype(BF16), lroots_v[1].astype(BF16), 1, 1)
        kt[1] = kt[1] - KERNEL_RATE * update

    steps = []
    tap_at = [0, 0]
    for k, n, kind in PIECES:
        compute = functools.partial(weights, k, tap_at[k], n)
        steps.append(iter(piece(k, tap_at[k] * chan, n * chan, kind, compute)))
        tap_at[k] += n
    passes = {
        -1: iter([functools.partial(add_back, 1, a) for a in range(3)]),
        -2: iter([pre_sums]),
        -3: iter([first_conv_grad]),
        -4: iter([functools.partial(add_back, 0, a) for a in range(3)]),
        -5: iter([board_grads]),
        -7: iter([second_left, lambda: (second_right(0), second_right(1)), lambda: second_right(2), second_kernel]),
    }
    for item in ORDER:
        next(steps[item] if item >= 0 else passes[item])()
    gain_one_sum, shift_one_sum = kept["sums"]

    norm_grad = [
        jnp.concatenate([gain_one_sum, shift_one_sum], axis=0),
        jnp.concatenate([gain_two_sum, shift_two_sum], axis=0),
    ]
    for k in range(2):
        value = MOMENTUM * mom[k] + norm_grad[k] * (1.0 / count)
        new_momenta[k] = value
        new_params[k] = par[k] - NORM_RATE * value

    for k, size, out_flag in sent:
        wait_for(gp.at[k, pl.ds(0, size)], out_flag)


def finish_kernel(
    dims,
    g_full,
    stats,
    roots,
    lstats,
    lroots,
    kt,
    bo,
    bg,
    momenta,
    params,
    o_block,
    o_board,
    o_grad,
    o_kernel,
    o_left,
    o_right,
    o_momenta,
    o_params,
    gb,
    nr,
    nk,
    nl,
    sem,
):
    chan = dims[3]
    chunk = 3 * chan
    share_width = kt.shape[1]
    start = pl.multiple_of(lax.axis_index("narrow") * share_width, 8)

    def put(slot, src, dst):
        pltpu.make_async_copy(src, dst, sem.at[slot]).start()

    put(0, stats.at[1], o_right.at[1])
    for k in range(2):
        put(1, g_full.at[k, pl.ds(start, share_width)], o_grad.at[k])
    put(2, kt.at[1], o_kernel.at[1])
    put(3, lstats.at[1], o_left.at[1])
    for i in range(SIDE):
        put(4, bo.at[i], o_block.at[:, i])
        put(5, bg.at[i], o_board.at[:, i])
    put(6, momenta, o_momenta)
    put(7, params, o_params)
    gb[...] = g_full[0].astype(BF16)
    own = g_full[0, pl.ds(start, share_width), :].astype(BF16)
    for q in range(3):
        cols = pl.ds(q * chunk, chunk)
        term = dot(own, gb[cols, :], 1, 1)
        nr[q] = STAT_DECAY * stats[0, :, cols] + (1.0 - STAT_DECAY) * term
        put(8, nr.at[q], o_right.at[0, :, cols])
    term = dot(gb[...], gb[...], 0, 0)
    nl[...] = STAT_DECAY * lstats[0] + (1.0 - STAT_DECAY) * term
    put(9, nl, o_left.at[0])
    mixed = dot(roots[0].astype(BF16), gb[...], 1, 0)
    update = dot(mixed.astype(BF16), lroots[0].astype(BF16), 1, 1)
    nk[...] = kt[0] - KERNEL_RATE * update
    put(10, nk, o_kernel.at[0])
    wholes = (stats.at[1], kt, nk, nl, bo, bg, momenta, params, nr, nl, nk)
    for slot, whole in enumerate(wholes):
        pltpu.make_async_copy(whole, whole, sem.at[slot]).wait()


def room_of(size, kind, extra):
    rows = 0
    for step in kind:
        size //= 4 if step == "z" else 2
        rows += 3 * size if step == "z" else size
    return rows + extra * size


def body(
    nw,
    nn,
    boards,
    history_mask,
    kernels,
    norm_params,
    norm_momenta,
    left_stats,
    right_stats,
    left_roots,
    right_roots,
    out_cotangent,
):
    pos, chan = boards.shape[0], boards.shape[3]
    kin = kernels.shape[2]
    share_width = right_stats.shape[2]
    line = pos * SIDE
    rows = line * SIDE
    chunk = 3 * chan
    ndev = nw * nn
    extra = max(nw.bit_length() - 4, 0)
    dims = (nw, nn, pos, chan)
    hbm = pl.BlockSpec(memory_space=pl.ANY)
    vmem = pl.BlockSpec(memory_space=pltpu.VMEM)
    board_shape = (SIDE, pos, SIDE, chan)

    kept = [
        (2, kin, chan),
        (2, share_width, kin),
        (2, share_width, kin),
        (2, chan, chan),
        (2, chan, chan),
        (2, share_width, chan),
        board_shape,
        board_shape,
        (2, 2, chan),
        (2, 2, chan),
    ]
    arrivals = max(
        sum(room_of(n * chan, kind, extra) for layer, n, kind in PIECES if layer == k)
        for k in range(2)
    )
    flags = sum(len(kind) + 1 + 2 * extra for _, _, kind in PIECES)
    room = (49 + extra) * MIB // 2 + (ndev - 32) * 8 * chan * 4 + 8 * chan * max(arrivals - kin, 0)
    fused = pl.pallas_call(
        functools.partial(fused_kernel, dims),
        out_shape=[pltpu.VMEM(shape, F32) for shape in kept],
        in_specs=[hbm] * 10,
        out_specs=[vmem] * len(kept),
        scratch_shapes=[
            pltpu.VMEM(board_shape, F32),
            pltpu.VMEM(board_shape, F32),
            pltpu.VMEM(history_mask.shape[::-1], jnp.int32),
            pltpu.VMEM((2, 2, chan), F32),
            pltpu.VMEM((2, 2, chan), F32),
            pltpu.VMEM((chan, kin), F32),
            pltpu.VMEM((2, chan, kin), BF16),
            pltpu.VMEM((rows + 2 * line, chunk), BF16),
            pltpu.VMEM((rows + 2 * line, chunk), BF16),
            pltpu.VMEM((rows + 2 * line, chunk), BF16),
            pltpu.VMEM((rows, chan), F32),
            pltpu.VMEM((rows, chan), F32),
            pltpu.VMEM((rows, chan), F32),
            pltpu.VMEM((rows, chan), F32),
            pltpu.VMEM((rows, chan), F32),
            pltpu.VMEM((2, kin, chan), F32),
            pltpu.VMEM((4, ndev, 2, chan), F32),
            pltpu.VMEM((2, arrivals, chan), F32),
            pltpu.SemaphoreType.DMA((13,)),
            pltpu.SemaphoreType.DMA((1,)),
            pltpu.SemaphoreType.DMA((2,)),
            pltpu.SemaphoreType.DMA((len(PIECES),)),
            pltpu.SemaphoreType.DMA((flags,)),
        ],
        compiler_params=pltpu.CompilerParams(
            collective_id=0, has_side_effects=True, vmem_limit_bytes=room
        ),
        name="fused_passes",
    )
    given = (
        boards,
        history_mask.T,
        kernels,
        norm_params,
        norm_momenta,
        left_stats,
        left_roots,
        jnp.swapaxes(right_stats, 1, 2),
        jnp.swapaxes(right_roots, 1, 2),
        out_cotangent,
    )
    held = fused(*(pltpu.with_memory_space_constraint(v, pltpu.HBM) for v in given))
    held = [pltpu.with_memory_space_constraint(v, pltpu.VMEM) for v in held]
    finish = pl.pallas_call(
        functools.partial(finish_kernel, dims),
        out_shape=[
            pltpu.HBM(boards.shape, F32),
            pltpu.HBM(boards.shape, F32),
            pltpu.HBM((2, share_width, chan), F32),
            pltpu.HBM((2, share_width, chan), F32),
            pltpu.HBM((2, chan, chan), F32),
            pltpu.HBM((2, share_width, kin), F32),
            pltpu.HBM((2, 2, chan), F32),
            pltpu.HBM((2, 2, chan), F32),
        ],
        in_specs=[vmem] * len(kept),
        out_specs=[hbm] * 8,
        scratch_shapes=[
            pltpu.VMEM((kin, chan), BF16),
            pltpu.VMEM((3, share_width, chunk), F32),
            pltpu.VMEM((share_width, chan), F32),
            pltpu.VMEM((chan, chan), F32),
            pltpu.SemaphoreType.DMA((11,)),
        ],
        compiler_params=pltpu.CompilerParams(vmem_limit_bytes=20 * MIB),
        name="finish",
    )
    block_out, board_grad, grad, kernel, left, right, momenta, params = finish(*held)
    return (
        block_out,
        board_grad,
        jnp.swapaxes(grad, 1, 2),
        jnp.swapaxes(kernel, 1, 2),
        left,
        jnp.swapaxes(right, 1, 2),
        momenta,
        params,
    )


def solution(mesh):
    nw, nn = mesh.shape["wide"], mesh.shape["narrow"]
    boards = P(("wide", "narrow"), None, None, None)
    columns = P(None, None, "narrow")
    in_specs = (
        boards,
        P(("wide", "narrow"), None),
        P(),
        P(),
        P(),
        P(),
        columns,
        P(),
        columns,
        boards,
    )
    out_specs = (boards, boards, columns, columns, P(), columns, P(), P())
    return jax.shard_map(
        functools.partial(body, nw, nn),
        mesh=mesh,
        in_specs=in_specs,
        out_specs=out_specs,
        check_vma=False,
    )
```

```python
import functools
import math

import jax
import jax.numpy as jnp
from jax import lax
from jax.experimental import pallas as pl
from jax.experimental.pallas import tpu as pltpu
from jax.sharding import PartitionSpec as P

EPS = 1e-05
MOMENTUM = 0.9
NORM_RATE = 50.0
KERNEL_RATE = 0.1
STAT_DECAY = 0.5

SIDE = 8
CUBE = 0.044715
ROOT = math.sqrt(2.0 / math.pi)
MESH = pl.DeviceIdType.MESH
F32 = jnp.float32
BF16 = jnp.bfloat16
MIB = 2**20


PIECES = (
    (1, 1, "c12z"), (1, 1, "c12ab"), (1, 1, "c12z"), (1, 1, "cab12"),
    (1, 1, "c12ab"), (1, 1, "c12ab"), (1, 1, "c12z"), (1, 1, "c12ab"),
    (1, 1, "cz12"), (0, 1, "c12z"), (0, 1, "c12ab"), (0, 1, "c12z"),
    (0, 1, "c12ab"), (0, 1, "cz12"), (0, 1, "c12z"), (0, 1, "c12z"),
    (0, 1, "c12z"), (0, 1, "c12ab"),
)
ORDER = (
    5, -1, -1, 4, -1, 5, -2, 7, 3, 4, 1, 6, 8, 0, 7, 3, 1, 6, 8, 0,
    5, 2, 2, 4, 7, -3, 13, 3, 17, 1, 10, 16, 5, 6, 13, 17, 0, 10, 15, 12,
    16, 7, 9, 2, 1, 5, 4, 6, 12, 8, 3, 0, 15, 17, 14, 7, 10, 9, 1, 2,
    16, 5, 11, 4, 14, 13, 12, 8, 6, 17, 11, 3, 0, 15, 7, 1, 10, 16, 9, 5,
    12, 2, 8, 14, 17, 4, 13, 3, 6, 15, 11, 10, 7, 1, 9, 5, 8, 12, 0, 14,
    3, 13, 16, 6, 4, 17, 2, 11, 7, 1, 10, 15, 5, 13, 0, 9, 12, 4, 14, 3,
    2, 16, 7, 17, -4, 11, 5, 1, 10, 6, 8, 15, 4, 9, 12, 16, 17, 14, 10, 3,
    15, -4, 13, 0, 11, 7, 9, 1, 4, 12, 5, 6, 0, 17, 1, 2, 14, 7, 4, -4,
    10, 8, 15, 11, 3, -5, 2, 12, 9, 3, 8, 16, 17, -7, -7, 10, 14, 13, -7, 11,
    12, 17, -7, 10, 13, 14, 16, 9, 15, 11, 12,
)


def dot(lhs, rhs, lhs_dim, rhs_dim):
    return lax.dot_general(
        lhs, rhs, (((lhs_dim,), (rhs_dim,)), ((), ())), preferred_element_type=F32
    )


def gelu_tanh(v):
    return jnp.tanh(ROOT * (v + CUBE * (v * v * v)))


def gelu_slope(v, t):
    inner = ROOT * (1.0 + (3.0 * CUBE) * (v * v))
    return 0.5 * (1.0 + t) + (0.5 * v) * ((1.0 - t * t) * inner)


def flip(index, bit):
    return index + (1 - 2 * ((index // (1 << bit)) % 2)) * (1 << bit)


def bit_of(index, bit):
    return (index // (1 << bit)) % 2


def pick(taken, one, other):
    return taken * one + (1 - taken) * other


def fused_kernel(
    dims,
    boards,
    mask_t,
    kernels,
    params,
    momenta,
    left_stats,
    left_roots,
    right_stats,
    right_roots,
    cotangent,
    g_full,
    stats_v,
    roots_v,
    lstats_v,
    lroots_v,
    kt,
    bo,
    bg,
    new_momenta,
    new_params,
    bd,
    ct,
    mk,
    par,
    mom,
    kf,
    wb,
    x_one,
    x_two,
    dgrid,
    h_one,
    slope_one,
    h_two,
    d_sum,
    d_hid,
    gp,
    red,
    arrived,
    load_sem,
    red_send,
    red_recv,
    g_send,
    g_recv,
):
    nw, nn, pos, chan = dims
    line = pos * SIDE
    rows = line * SIDE
    count = float(rows * nw * nn)
    chunk = 3 * chan
    wide, narrow = lax.axis_index("wide"), lax.axis_index("narrow")
    me = wide * nn + narrow
    extra_bits = list(range(3, nw.bit_length() - 1))

    def load(slot, src, dst):
        copy = pltpu.make_async_copy(src, dst, load_sem.at[slot])
        copy.start()
        return copy

    got_mask = load(0, mask_t, mk)
    for i in range(SIDE):
        load(1, boards.at[:, i], bd.at[i])
    got_k0 = [
        load(9 + a, kernels.at[0, :, pl.ds(a * chunk, chunk)], kf.at[:, pl.ds(a * chunk, chunk)])
        for a in range(3)
    ]
    got_par = load(3, params, par)

    def each_other(act):
        if nw * nn <= 32:
            for k in range(nw * nn - 1, 0, -1):
                w, n = wide, narrow
                for b in range(nw.bit_length() - 1):
                    if (k // nn) >> b & 1:
                        w = flip(w, b) if b == 0 else w + (flip(wide, b) - wide)
                for b in range(nn.bit_length() - 1):
                    if (k % nn) >> b & 1:
                        n = n + (flip(narrow, b) - narrow)
                act((w, n))
        else:

            @pl.loop(1, nw * nn)
            def _(k):
                other = lax.rem(me + k, nw * nn)
                act((other // nn, lax.rem(other, nn)))

    barrier = pltpu.get_barrier_semaphore()
    each_other(
        lambda dev: pl.semaphore_signal(barrier, inc=1, device_id=dev, device_id_type=MESH)
    )

    def share(slot, value):
        red[slot, me] = value

        def send(dev):
            pltpu.make_async_remote_copy(
                src_ref=red.at[slot, me],
                dst_ref=red.at[slot, me],
                send_sem=red_send.at[0],
                recv_sem=red_recv.at[slot % 2],
                device_id=dev,
                device_id_type=MESH,
            ).start()

        each_other(send)

    def collect(slot):
        others = red.at[slot, pl.ds(0, nw * nn - 1)]
        pltpu.make_async_copy(others, others, red_recv.at[slot % 2]).wait()
        pltpu.make_async_copy(others, others, red_send.at[0]).wait()
        return red[slot]

    def moments(slot):
        got = collect(slot)
        means, spreads = got[:, 0, :], got[:, 1, :]
        mean = jnp.sum(means, axis=0, keepdims=True) * (1.0 / (nw * nn))
        gap = means - mean
        spread = jnp.sum(spreads, axis=0, keepdims=True) + float(rows) * jnp.sum(
            gap * gap, axis=0, keepdims=True
        )
        return mean, lax.rsqrt(spread / count + EPS)

    def totals(slot):
        got = collect(slot)
        return (
            jnp.sum(got[:, 0, :], axis=0, keepdims=True),
            jnp.sum(got[:, 1, :], axis=0, keepdims=True),
        )

    def local_moments(ref):
        total = jnp.sum(ref[...], axis=0, keepdims=True)
        mean = total * (1.0 / rows)
        gap = ref[...] - mean
        return jnp.concatenate([mean, jnp.sum(gap * gap, axis=0, keepdims=True)], axis=0)

    column = lax.broadcasted_iota(jnp.int32, (pos, SIDE, chan), 1)

    def put_shifted(grid, i, value):
        cube = value.reshape(pos, SIDE, chan)
        before = jnp.where(column == 0, 0.0, pltpu.roll(cube, 1, 1))
        after = jnp.where(column == SIDE - 1, 0.0, pltpu.roll(cube, SIDE - 1, 1))
        at = pl.ds(pl.multiple_of((i + 1) * line, 16), line)
        grid[at, 0:chan] = before.reshape(line, chan).astype(BF16)
        grid[at, chan : 2 * chan] = value.astype(BF16)
        grid[at, 2 * chan : 3 * chan] = after.reshape(line, chan).astype(BF16)

    def at_line(i):
        return pl.ds(pl.multiple_of(i * line, 8), line)

    def conv(grid, k, result):
        tile = rows // 2

        @pl.loop(0, 2)
        def _(i):
            result[pl.ds(pl.multiple_of(i * tile, 8), tile), :] = sum(
                dot(
                    grid[pl.ds(pl.multiple_of(a * line + i * tile, 16), tile), :],
                    wb[k, :, a * chunk : (a + 1) * chunk],
                    1,
                    1,
                )
                for a in range(3)
            )

    def conv_back(grid, k, a):
        result = None
        for b in range(3):
            tap = 3 * (2 - a) + (2 - b)
            term = dot(
                grid[a * line : a * line + rows, b * chan : (b + 1) * chan],
                wb[k, :, tap * chan : (tap + 1) * chan],
                1,
                0,
            )
            result = term if result is None else result + term
        return result

    core = bit_of(narrow, 0)
    x_bit, y_bit = bit_of(narrow, 1), bit_of(wide, 0)
    z_low, z_high = bit_of(wide, 1), bit_of(wide, 2)
    z_pos = z_low + 2 * z_high
    x_dev = (wide, flip(narrow, 1))
    y_dev = (flip(wide, 0), narrow)
    pairs = {
        "c": ((wide, flip(narrow, 0)), core),
        "1": (
            (pick(core, y_dev[0], x_dev[0]), pick(core, y_dev[1], x_dev[1])),
            pick(core, y_bit, x_bit),
        ),
        "2": (
            (pick(core, x_dev[0], y_dev[0]), pick(core, x_dev[1], y_dev[1])),
            pick(core, x_bit, y_bit),
        ),
        "a": ((flip(wide, 1), narrow), z_low),
        "b": ((flip(wide, 2), narrow), z_high),
    }
    line_devs = []
    for q in (3, 2, 1):
        other = (1 - z_low if q & 1 else z_low) + 2 * (1 - z_high if q & 2 else z_high)
        line_devs.append((other, (wide + 2 * (other - z_pos), narrow)))

    filled = [0, 0]
    flags = iter(range(g_recv.shape[0]))
    sent = []

    def remote(src, dst, dev, send_sem, recv_sem):
        pltpu.make_async_remote_copy(
            src_ref=src,
            dst_ref=dst,
            send_sem=send_sem,
            recv_sem=recv_sem,
            device_id=dev,
            device_id_type=MESH,
        ).start()

    def wait_for(ref, sem):
        pltpu.make_async_copy(ref, ref, sem).wait()

    def at(start, size):
        return pl.ds(pl.multiple_of(start, 8), size)

    def piece(k, base, size, kind, compute):
        starts, sizes, into = [base], [size], []
        for step in kind:
            place = z_pos if step == "z" else pairs[step][1]
            sizes.append(sizes[-1] // (4 if step == "z" else 2))
            starts.append(starts[-1] + place * sizes[-1])
        last = len(kind) - 1
        own = at(starts[-1], sizes[-1])
        flag = [g_recv.at[next(flags)] for _ in kind]
        back_flag = [g_recv.at[next(flags)]] + flag[:-1]
        out_flag = g_send.at[len(sent)]
        sent.append((k, 2 * (size - sizes[-1]), out_flag))

        def scatter(i):
            part = sizes[i + 1]
            if kind[i] == "z":
                targets = line_devs
            else:
                dev, place = pairs[kind[i]]
                targets = [(1 - place, dev)]
            start = filled[k]
            into.append((start, part * len(targets)))
            filled[k] += part * len(targets)
            for q, (place, dev) in enumerate(targets):
                src = gp.at[k, at(starts[i] + place * part, part)]
                dst = arrived.at[k, pl.ds(start + q * part, part)]
                remote(src, dst, dev, out_flag, flag[i])

        def add(i):
            part = sizes[i + 1]
            start, total = into[i]
            wait_for(arrived.at[k, pl.ds(start, total)], flag[i])
            rows_here = at(starts[i + 1], part)
            value = gp[k, rows_here]
            for q in range(total // part):
                value = value + arrived[k, start + q * part : start + (q + 1) * part]
            return rows_here, value

        def gather(i):
            ref = g_full.at[k, at(starts[i + 1], sizes[i + 1])]
            targets = line_devs if kind[i] == "z" else [(0, pairs[kind[i]][0])]
            for _, dev in targets:
                remote(ref, ref, dev, out_flag, back_flag[i])

        def start():
            compute()
            scatter(0)

        def middle(i):
            rows_here, value = add(i)
            gp[k, rows_here] = value
            scatter(i + 1)

        def turn():
            _, value = add(last)
            for b in extra_bits:
                gp[k, own] = value
                into_more = arrived.at[k, pl.ds(filled[k], sizes[-1])]
                more = g_recv.at[next(flags)], g_recv.at[next(flags)]
                remote(gp.at[k, own], into_more, (flip(wide, b), narrow), *more)
                wait_for(into_more, more[0])
                wait_for(into_more, more[1])
                value = value + arrived[k, filled[k] : filled[k] + sizes[-1]]
                filled[k] += sizes[-1]
            g_full[k, own] = value * (1.0 / count)
            gather(last)

        def back(i):
            got = (3 if kind[i] == "z" else 1) * sizes[i + 1]
            wait_for(g_full.at[k, pl.ds(base, got)], back_flag[i])
            if i:
                gather(i - 1)

        return (
            [start]
            + [functools.partial(middle, i) for i in range(last)]
            + [turn]
            + [functools.partial(back, i) for i in range(last, -1, -1)]
        )

    def clear_ends(grid):
        empty = jnp.zeros((line, 3 * chan), BF16)
        grid[0:line, :] = empty
        grid[line + rows : 2 * line + rows, :] = empty

    clear_ends(x_one)
    got_mask.wait()
    hist = mk.shape[0]
    width = chan // hist
    spot = lax.broadcasted_iota(jnp.int32, (pos, line), 1)
    owner = SIDE * lax.broadcasted_iota(jnp.int32, (pos, line), 0)
    spread_pos = jnp.where((spot >= owner) & (spot < owner + SIDE), 1.0, 0.0).astype(BF16)
    spot = lax.broadcasted_iota(jnp.int32, (hist, chan), 1)
    owner = width * lax.broadcasted_iota(jnp.int32, (hist, chan), 0)
    spread_chan = jnp.where((spot >= owner) & (spot < owner + width), 1.0, 0.0).astype(BF16)
    by_row = dot(mk[...].astype(F32).astype(BF16), spread_pos, 1, 0).astype(BF16)
    planes = dot(by_row, spread_chan, 0, 0)

    pltpu.make_async_copy(bd, bd, load_sem.at[1]).wait()
    for i in range(SIDE):
        value = bd[i].reshape(line, chan) * planes
        bd[i] = value.reshape(pos, SIDE, chan)
        put_shifted(x_one, i, value)

    for a in range(3):
        got_k0[a].wait()
        part = slice(a * chunk, (a + 1) * chunk)
        wb[0, :, part] = kf[:, part].astype(BF16)
    conv(x_one, 0, h_one)
    local = local_moments(h_one)
    pl.semaphore_wait(barrier, nw * nn - 1)
    share(0, local)

    got_par.wait()

    def keep_share(k):
        share_width = kt.shape[1]
        span = -(-(share_width + 64) // 128) * 128
        start = narrow * share_width
        block = (start // 128) * 128
        d_hid[0:span, :] = kf[:, pl.ds(pl.multiple_of(block, 128), span)].T
        kt[k] = d_hid[pl.ds(pl.multiple_of(start - block, 8), share_width), :]

    clear_ends(x_two)
    clear_ends(dgrid)
    keep_share(0)
    got_k1 = load(4, kernels.at[1], kf)
    for i in range(SIDE):
        load(5, cotangent.at[:, i], ct.at[i])
    late = [
        load(6, momenta, mom),
        load(7, left_stats, lstats_v),
        load(8, left_roots, lroots_v),
        load(12, right_roots, roots_v),
        load(2, right_stats, stats_v),
    ]
    got_k1.wait()
    wb[1] = kf[...].astype(BF16)
    keep_share(1)

    gain_one, shift_one = par[0, 0:1, :], par[0, 1:2, :]
    gain_two, shift_two = par[1, 0:1, :], par[1, 1:2, :]

    mean_one, inv_one = moments(0)

    @pl.loop(0, SIDE)
    def _(i):
        at = at_line(i)
        normed = (h_one[at, :] - mean_one) * inv_one
        h_one[at, :] = normed
        pre = normed * gain_one + shift_one
        put_shifted(x_two, i, (0.5 * pre) * (1.0 + gelu_tanh(pre)))

    conv(x_two, 1, h_two)
    share(1, local_moments(h_two))

    @pl.loop(0, SIDE)
    def _(i):
        at = at_line(i)
        pre = h_one[at, :] * gain_one + shift_one
        slope_one[at, :] = gelu_slope(pre, gelu_tanh(pre))

    pltpu.make_async_copy(ct, ct, load_sem.at[5]).wait()
    mean_two, inv_two = moments(1)

    def fold(value):
        return jnp.sum(value.reshape(pos, SIDE, chan), axis=0)

    nothing = jnp.zeros((SIDE, chan), F32)

    def close(gain_sum, shift_sum):
        return jnp.concatenate(
            [
                jnp.sum(gain_sum, axis=0, keepdims=True),
                jnp.sum(shift_sum, axis=0, keepdims=True),
            ],
            axis=0,
        )

    def out_line(i, carry):
        at = at_line(i)
        normed = (h_two[at, :] - mean_two) * inv_two
        h_two[at, :] = normed
        summed = bd[i].reshape(line, chan) + normed * gain_two + shift_two
        t = gelu_tanh(summed)
        bo[i] = ((0.5 * summed) * (1.0 + t)).reshape(pos, SIDE, chan)
        slope = ct[i].reshape(line, chan) * gelu_slope(summed, t)
        d_sum[at, :] = slope
        return carry[0] + fold(slope * normed), carry[1] + fold(slope)

    share(2, close(*lax.fori_loop(0, SIDE, out_line, (nothing, nothing))))

    gain_two_sum, shift_two_sum = totals(2)
    scale_two = gain_two * inv_two

    @pl.loop(0, SIDE)
    def _(i):
        at = at_line(i)
        lost = (shift_two_sum + h_two[at, :] * gain_two_sum) * (1.0 / count)
        put_shifted(dgrid, i, scale_two * (d_sum[at, :] - lost))

    def weights(k, first, taps_here):
        grid = (x_one, x_two)[k]
        tap = first
        while tap < first + taps_here:
            a, b = divmod(tap, 3)
            n = min(3 - b, first + taps_here - tap)
            g_part = dot(
                grid[a * line : a * line + rows, b * chan : (b + n) * chan],
                dgrid[line : line + rows, chan : 2 * chan],
                0,
                0,
            )
            gp[k, tap * chan : (tap + n) * chan, :] = g_part
            tap += n

    def add_back(k, a):
        term = conv_back(dgrid, k, a)
        d_hid[...] = d_hid[...] + term if a else term

    kept = {}

    def pre_sums():
        def pre_line(i, carry):
            at = at_line(i)
            d_pre = d_hid[at, :] * slope_one[at, :]
            d_hid[at, :] = d_pre
            return carry[0] + fold(d_pre * h_one[at, :]), carry[1] + fold(d_pre)

        share(3, close(*lax.fori_loop(0, SIDE, pre_line, (nothing, nothing))))

    def first_conv_grad():
        kept["sums"] = gain_one_sum, shift_one_sum = totals(3)
        scale_one = gain_one * inv_one

        @pl.loop(0, SIDE)
        def _(i):
            at = at_line(i)
            lost = (shift_one_sum + h_one[at, :] * gain_one_sum) * (1.0 / count)
            put_shifted(dgrid, i, scale_one * (d_hid[at, :] - lost))

    def board_grads():
        for i in range(SIDE):
            at = at_line(i)
            bg[i] = ((d_sum[at, :] + d_hid[at, :]) * planes).reshape(pos, SIDE, chan)

    def second_left():
        for copy in late:
            copy.wait()
        for a in range(3):
            x_two[0:chunk, a * chan : (a + 1) * chan] = g_full[
                1, a * chunk : (a + 1) * chunk, :
            ].astype(BF16)
        blocks = [x_two[0:chunk, a * chan : (a + 1) * chan] for a in range(3)]
        term = sum(dot(block, block, 0, 0) for block in blocks)
        lstats_v[1] = STAT_DECAY * lstats_v[1] + (1.0 - STAT_DECAY) * term

    def second_right(a):
        width = kt.shape[1]
        start = pl.multiple_of(narrow * width, 8)
        own = g_full[1, pl.ds(start, width), :].astype(BF16)
        cols = slice(a * chunk, (a + 1) * chunk)
        term = dot(own, x_two[0:chunk, a * chan : (a + 1) * chan], 1, 1)
        stats_v[1, :, cols] = STAT_DECAY * stats_v[1, :, cols] + (1.0 - STAT_DECAY) * term

    def second_kernel():
        mixed = sum(
            dot(
                roots_v[1, :, a * chunk : (a + 1) * chunk].astype(BF16),
                x_two[0:chunk, a * chan : (a + 1) * chan],
                1,
                0,
            )
            for a in range(3)
        )
        update = dot(mixed.astype(BF16), lroots_v[1].astype(BF16), 1, 1)
        kt[1] = kt[1] - KERNEL_RATE * update

    steps = []
    tap_at = [0, 0]
    for k, n, kind in PIECES:
        compute = functools.partial(weights, k, tap_at[k], n)
        steps.append(iter(piece(k, tap_at[k] * chan, n * chan, kind, compute)))
        tap_at[k] += n
    passes = {
        -1: iter([functools.partial(add_back, 1, a) for a in range(3)]),
        -2: iter([pre_sums]),
        -3: iter([first_conv_grad]),
        -4: iter([functools.partial(add_back, 0, a) for a in range(3)]),
        -5: iter([board_grads]),
        -7: iter([second_left, lambda: (second_right(0), second_right(1)), lambda: second_right(2), second_kernel]),
    }
    for item in ORDER:
        next(steps[item] if item >= 0 else passes[item])()
    gain_one_sum, shift_one_sum = kept["sums"]

    norm_grad = [
        jnp.concatenate([gain_one_sum, shift_one_sum], axis=0),
        jnp.concatenate([gain_two_sum, shift_two_sum], axis=0),
    ]
    for k in range(2):
        value = MOMENTUM * mom[k] + norm_grad[k] * (1.0 / count)
        new_momenta[k] = value
        new_params[k] = par[k] - NORM_RATE * value

    for k, size, out_flag in sent:
        wait_for(gp.at[k, pl.ds(0, size)], out_flag)


def finish_kernel(
    dims,
    g_full,
    stats,
    roots,
    lstats,
    lroots,
    kt,
    bo,
    bg,
    momenta,
    params,
    o_block,
    o_board,
    o_grad,
    o_kernel,
    o_left,
    o_right,
    o_momenta,
    o_params,
    gb,
    nr,
    nk,
    nl,
    sem,
):
    chan = dims[3]
    chunk = 3 * chan
    share_width = kt.shape[1]
    start = pl.multiple_of(lax.axis_index("narrow") * share_width, 8)

    def put(slot, src, dst):
        pltpu.make_async_copy(src, dst, sem.at[slot]).start()

    put(0, stats.at[1], o_right.at[1])
    for k in range(2):
        put(1, g_full.at[k, pl.ds(start, share_width)], o_grad.at[k])
    put(2, kt.at[1], o_kernel.at[1])
    put(3, lstats.at[1], o_left.at[1])
    for i in range(SIDE):
        put(4, bo.at[i], o_block.at[:, i])
        put(5, bg.at[i], o_board.at[:, i])
    put(6, momenta, o_momenta)
    put(7, params, o_params)
    gb[...] = g_full[0].astype(BF16)
    own = g_full[0, pl.ds(start, share_width), :].astype(BF16)
    for q in range(3):
        cols = pl.ds(q * chunk, chunk)
        term = dot(own, gb[cols, :], 1, 1)
        nr[q] = STAT_DECAY * stats[0, :, cols] + (1.0 - STAT_DECAY) * term
        put(8, nr.at[q], o_right.at[0, :, cols])
    term = dot(gb[...], gb[...], 0, 0)
    nl[...] = STAT_DECAY * lstats[0] + (1.0 - STAT_DECAY) * term
    put(9, nl, o_left.at[0])
    mixed = dot(roots[0].astype(BF16), gb[...], 1, 0)
    update = dot(mixed.astype(BF16), lroots[0].astype(BF16), 1, 1)
    nk[...] = kt[0] - KERNEL_RATE * update
    put(10, nk, o_kernel.at[0])
    wholes = (stats.at[1], kt, nk, nl, bo, bg, momenta, params, nr, nl, nk)
    for slot, whole in enumerate(wholes):
        pltpu.make_async_copy(whole, whole, sem.at[slot]).wait()


def room_of(size, kind, extra):
    rows = 0
    for step in kind:
        size //= 4 if step == "z" else 2
        rows += 3 * size if step == "z" else size
    return rows + extra * size


def body(
    nw,
    nn,
    boards,
    history_mask,
    kernels,
    norm_params,
    norm_momenta,
    left_stats,
    right_stats,
    left_roots,
    right_roots,
    out_cotangent,
):
    pos, chan = boards.shape[0], boards.shape[3]
    kin = kernels.shape[2]
    share_width = right_stats.shape[2]
    line = pos * SIDE
    rows = line * SIDE
    chunk = 3 * chan
    ndev = nw * nn
    extra = max(nw.bit_length() - 4, 0)
    dims = (nw, nn, pos, chan)
    hbm = pl.BlockSpec(memory_space=pl.ANY)
    vmem = pl.BlockSpec(memory_space=pltpu.VMEM)
    board_shape = (SIDE, pos, SIDE, chan)

    kept = [
        (2, kin, chan),
        (2, share_width, kin),
        (2, share_width, kin),
        (2, chan, chan),
        (2, chan, chan),
        (2, share_width, chan),
        board_shape,
        board_shape,
        (2, 2, chan),
        (2, 2, chan),
    ]
    arrivals = max(
        sum(room_of(n * chan, kind, extra) for layer, n, kind in PIECES if layer == k)
        for k in range(2)
    )
    flags = sum(len(kind) + 1 + 2 * extra for _, _, kind in PIECES)
    room = (49 + extra) * MIB // 2 + (ndev - 32) * 8 * chan * 4 + 8 * chan * max(arrivals - kin, 0)
    fused = pl.pallas_call(
        functools.partial(fused_kernel, dims),
        out_shape=[pltpu.VMEM(shape, F32) for shape in kept],
        in_specs=[hbm] * 10,
        out_specs=[vmem] * len(kept),
        scratch_shapes=[
            pltpu.VMEM(board_shape, F32),
            pltpu.VMEM(board_shape, F32),
            pltpu.VMEM(history_mask.shape[::-1], jnp.int32),
            pltpu.VMEM((2, 2, chan), F32),
            pltpu.VMEM((2, 2, chan), F32),
            pltpu.VMEM((chan, kin), F32),
            pltpu.VMEM((2, chan, kin), BF16),
            pltpu.VMEM((rows + 2 * line, chunk), BF16),
            pltpu.VMEM((rows + 2 * line, chunk), BF16),
            pltpu.VMEM((rows + 2 * line, chunk), BF16),
            pltpu.VMEM((rows, chan), F32),
            pltpu.VMEM((rows, chan), F32),
            pltpu.VMEM((rows, chan), F32),
            pltpu.VMEM((rows, chan), F32),
            pltpu.VMEM((rows, chan), F32),
            pltpu.VMEM((2, kin, chan), F32),
            pltpu.VMEM((4, ndev, 2, chan), F32),
            pltpu.VMEM((2, arrivals, chan), F32),
            pltpu.SemaphoreType.DMA((13,)),
            pltpu.SemaphoreType.DMA((1,)),
            pltpu.SemaphoreType.DMA((2,)),
            pltpu.SemaphoreType.DMA((len(PIECES),)),
            pltpu.SemaphoreType.DMA((flags,)),
        ],
        compiler_params=pltpu.CompilerParams(
            collective_id=0, has_side_effects=True, vmem_limit_bytes=room
        ),
        name="fused_passes",
    )
    given = (
        boards,
        history_mask.T,
        kernels,
        norm_params,
        norm_momenta,
        left_stats,
        left_roots,
        jnp.swapaxes(right_stats, 1, 2),
        jnp.swapaxes(right_roots, 1, 2),
        out_cotangent,
    )
    held = fused(*(pltpu.with_memory_space_constraint(v, pltpu.HBM) for v in given))
    held = [pltpu.with_memory_space_constraint(v, pltpu.VMEM) for v in held]
    finish = pl.pallas_call(
        functools.partial(finish_kernel, dims),
        out_shape=[
            pltpu.HBM(boards.shape, F32),
            pltpu.HBM(boards.shape, F32),
            pltpu.HBM((2, share_width, chan), F32),
            pltpu.HBM((2, share_width, chan), F32),
            pltpu.HBM((2, chan, chan), F32),
            pltpu.HBM((2, share_width, kin), F32),
            pltpu.HBM((2, 2, chan), F32),
            pltpu.HBM((2, 2, chan), F32),
        ],
        in_specs=[vmem] * len(kept),
        out_specs=[hbm] * 8,
        scratch_shapes=[
            pltpu.VMEM((kin, chan), BF16),
            pltpu.VMEM((3, share_width, chunk), F32),
            pltpu.VMEM((share_width, chan), F32),
            pltpu.VMEM((chan, chan), F32),
            pltpu.SemaphoreType.DMA((11,)),
        ],
        compiler_params=pltpu.CompilerParams(vmem_limit_bytes=20 * MIB),
        name="finish",
    )
    block_out, board_grad, grad, kernel, left, right, momenta, params = finish(*held)
    return (
        block_out,
        board_grad,
        jnp.swapaxes(grad, 1, 2),
        jnp.swapaxes(kernel, 1, 2),
        left,
        jnp.swapaxes(right, 1, 2),
        momenta,
        params,
    )


def solution(mesh):
    nw, nn = mesh.shape["wide"], mesh.shape["narrow"]
    boards = P(("wide", "narrow"), None, None, None)
    columns = P(None, None, "narrow")
    in_specs = (
        boards,
        P(("wide", "narrow"), None),
        P(),
        P(),
        P(),
        P(),
        columns,
        P(),
        columns,
        boards,
    )
    out_specs = (boards, boards, columns, columns, P(), columns, P(), P())
    return jax.shard_map(
        functools.partial(body, nw, nn),
        mesh=mesh,
        in_specs=in_specs,
        out_specs=out_specs,
        check_vma=False,
    )
```

```python
import functools
import math

import jax
import jax.numpy as jnp
from jax import lax
from jax.experimental import pallas as pl
from jax.experimental.pallas import tpu as pltpu
from jax.sharding import PartitionSpec as P

EPS = 1e-05
MOMENTUM = 0.9
NORM_RATE = 50.0
KERNEL_RATE = 0.1
STAT_DECAY = 0.5

SIDE = 8
CUBE = 0.044715
ROOT = math.sqrt(2.0 / math.pi)
MESH = pl.DeviceIdType.MESH
F32 = jnp.float32
BF16 = jnp.bfloat16
MIB = 2**20


PIECES = (
    (1, 1, "c12z"), (1, 1, "c12ab"), (1, 1, "c12z"), (1, 1, "cab12"),
    (1, 1, "c12ab"), (1, 1, "c12ab"), (1, 1, "c12z"), (1, 1, "c12ab"),
    (1, 1, "cz12"), (0, 1, "c12z"), (0, 1, "c12ab"), (0, 1, "c12z"),
    (0, 1, "c12ab"), (0, 1, "cz12"), (0, 1, "c12z"), (0, 1, "c12z"),
    (0, 1, "c12z"), (0, 1, "c12ab"),
)
ORDER = (
    5, -1, -1, 4, -1, 5, -2, 7, 3, 4, 1, 6, 8, 0, 7, 3, 1, 6, 8, 0,
    5, 2, 2, 4, 7, -3, 13, 3, 17, 1, 10, 16, 5, 6, 13, 17, 0, 10, 15, 12,
    16, 7, 9, 2, 1, 5, 4, 6, 12, 8, 3, 0, 15, 17, 14, 7, 10, 9, 1, 2,
    16, 5, 11, 4, 14, 13, 12, 8, 6, 17, 11, 3, 0, 15, 7, 1, 10, 16, 9, 5,
    12, 2, 8, 14, 17, 4, 13, 3, 6, 15, 11, 10, 7, 1, 9, 5, 8, 12, 0, 14,
    3, 13, 16, 6, 4, 17, 2, 11, 7, 1, 10, 15, 5, 13, 0, 9, 12, 4, 14, 3,
    2, 16, 7, 17, -4, 11, 5, 1, 10, 6, 8, 15, 4, 9, 12, 16, 17, 14, 10, 3,
    15, -4, 13, 0, 11, 7, 9, 1, 4, 12, 5, 6, 0, 17, 1, 2, 14, 7, 4, -4,
    10, 8, 15, 11, 3, -5, 2, 12, 9, 3, 8, 16, 17, -7, -7, 10, 14, 13, -7, 11,
    12, 17, -7, 10, 13, 14, 16, 9, 15, 11, 12,
)


def dot(lhs, rhs, lhs_dim, rhs_dim):
    return lax.dot_general(
        lhs, rhs, (((lhs_dim,), (rhs_dim,)), ((), ())), preferred_element_type=F32
    )


def gelu_tanh(v):
    return jnp.tanh(ROOT * (v + CUBE * (v * v * v)))


def gelu_slope(v, t):
    inner = ROOT * (1.0 + (3.0 * CUBE) * (v * v))
    return 0.5 * (1.0 + t) + (0.5 * v) * ((1.0 - t * t) * inner)


def flip(index, bit):
    return index + (1 - 2 * ((index // (1 << bit)) % 2)) * (1 << bit)


def bit_of(index, bit):
    return (index // (1 << bit)) % 2


def pick(taken, one, other):
    return taken * one + (1 - taken) * other


def fused_kernel(
    dims,
    boards,
    mask_t,
    kernels,
    params,
    momenta,
    left_stats,
    left_roots,
    right_stats,
    right_roots,
    cotangent,
    g_full,
    stats_v,
    roots_v,
    lstats_v,
    lroots_v,
    kt,
    bo,
    bg,
    new_momenta,
    new_params,
    bd,
    ct,
    mk,
    par,
    mom,
    kf,
    wb,
    x_one,
    x_two,
    dgrid,
    h_one,
    slope_one,
    h_two,
    d_sum,
    d_hid,
    gp,
    red,
    arrived,
    load_sem,
    red_send,
    red_recv,
    g_send,
    g_recv,
):
    nw, nn, pos, chan = dims
    line = pos * SIDE
    rows = line * SIDE
    count = float(rows * nw * nn)
    chunk = 3 * chan
    kin = 9 * chan
    wide, narrow = lax.axis_index("wide"), lax.axis_index("narrow")
    me = wide * nn + narrow
    extra_bits = list(range(3, nw.bit_length() - 1))

    def load(slot, src, dst):
        copy = pltpu.make_async_copy(src, dst, load_sem.at[slot])
        copy.start()
        return copy

    got_mask = load(0, mask_t, mk)
    for i in range(SIDE):
        load(1, boards.at[:, i], bd.at[i])
    got_k0 = [
        load(9 + a, kernels.at[0, :, pl.ds(a * chunk, chunk)], kf.at[:, pl.ds(a * chunk, chunk)])
        for a in range(3)
    ]
    got_par = load(3, params, par)

    def each_other(act):
        if nw * nn <= 32:
            for k in range(nw * nn - 1, 0, -1):
                w, n = wide, narrow
                for b in range(nw.bit_length() - 1):
                    if (k // nn) >> b & 1:
                        w = flip(w, b) if b == 0 else w + (flip(wide, b) - wide)
                for b in range(nn.bit_length() - 1):
                    if (k % nn) >> b & 1:
                        n = n + (flip(narrow, b) - narrow)
                act((w, n))
        else:

            @pl.loop(1, nw * nn)
            def _(k):
                other = lax.rem(me + k, nw * nn)
                act((other // nn, lax.rem(other, nn)))

    barrier = pltpu.get_barrier_semaphore()
    each_other(
        lambda dev: pl.semaphore_signal(barrier, inc=1, device_id=dev, device_id_type=MESH)
    )

    def share(slot, value):
        red[slot, me] = value
        if slot:
            sent_all(slot - 1)

        def send(dev):
            pltpu.make_async_remote_copy(
                src_ref=red.at[slot, me],
                dst_ref=red.at[slot, me],
                send_sem=red_send.at[0],
                recv_sem=red_recv.at[slot % 2],
                device_id=dev,
                device_id_type=MESH,
            ).start()

        each_other(send)

    def collect(slot):
        others = red.at[slot, pl.ds(0, nw * nn - 1)]
        pltpu.make_async_copy(others, others, red_recv.at[slot % 2]).wait()
        return red[slot]

    def sent_all(slot):
        others = red.at[slot, pl.ds(0, nw * nn - 1)]
        pltpu.make_async_copy(others, others, red_send.at[0]).wait()

    def moments(slot):
        got = collect(slot)
        means, spreads = got[:, 0, :], got[:, 1, :]
        mean = jnp.sum(means, axis=0, keepdims=True) * (1.0 / (nw * nn))
        gap = means - mean
        spread = jnp.sum(spreads, axis=0, keepdims=True) + float(rows) * jnp.sum(
            gap * gap, axis=0, keepdims=True
        )
        return mean, lax.rsqrt(spread / count + EPS)

    def totals(slot):
        got = collect(slot)
        return (
            jnp.sum(got[:, 0, :], axis=0, keepdims=True),
            jnp.sum(got[:, 1, :], axis=0, keepdims=True),
        )

    def local_moments(ref):
        total = jnp.sum(ref[...], axis=0, keepdims=True)
        mean = total * (1.0 / rows)
        gap = ref[...] - mean
        return jnp.concatenate([mean, jnp.sum(gap * gap, axis=0, keepdims=True)], axis=0)

    column = lax.broadcasted_iota(jnp.int32, (pos, SIDE, chan), 1)

    def put_shifted(grid, i, value):
        cube = value.reshape(pos, SIDE, chan)
        before = jnp.where(column == 0, 0.0, pltpu.roll(cube, 1, 1))
        after = jnp.where(column == SIDE - 1, 0.0, pltpu.roll(cube, SIDE - 1, 1))
        at = pl.ds(pl.multiple_of((i + 1) * line, 16), line)
        grid[at, 0:chan] = before.reshape(line, chan).astype(BF16)
        grid[at, chan : 2 * chan] = value.astype(BF16)
        grid[at, 2 * chan : 3 * chan] = after.reshape(line, chan).astype(BF16)

    def at_line(i):
        return pl.ds(pl.multiple_of(i * line, 8), line)

    def conv(grid, k, result):
        tile = rows // 2

        @pl.loop(0, 2)
        def _(i):
            result[pl.ds(pl.multiple_of(i * tile, 8), tile), :] = sum(
                dot(
                    grid[pl.ds(pl.multiple_of(a * line + i * tile, 16), tile), :],
                    wb[k, :, a * chunk : (a + 1) * chunk],
                    1,
                    1,
                )
                for a in range(3)
            )

    def conv_back(grid, k, a):
        result = None
        for b in range(3):
            tap = 3 * (2 - a) + (2 - b)
            term = dot(
                grid[a * line : a * line + rows, b * chan : (b + 1) * chan],
                wb[k, :, tap * chan : (tap + 1) * chan],
                1,
                0,
            )
            result = term if result is None else result + term
        return result

    core = bit_of(narrow, 0)
    x_bit, y_bit = bit_of(narrow, 1), bit_of(wide, 0)
    z_low, z_high = bit_of(wide, 1), bit_of(wide, 2)
    z_pos = z_low + 2 * z_high
    x_dev = (wide, flip(narrow, 1))
    y_dev = (flip(wide, 0), narrow)
    pairs = {
        "c": ((wide, flip(narrow, 0)), core),
        "1": (
            (pick(core, y_dev[0], x_dev[0]), pick(core, y_dev[1], x_dev[1])),
            pick(core, y_bit, x_bit),
        ),
        "2": (
            (pick(core, x_dev[0], y_dev[0]), pick(core, x_dev[1], y_dev[1])),
            pick(core, x_bit, y_bit),
        ),
        "a": ((flip(wide, 1), narrow), z_low),
        "b": ((flip(wide, 2), narrow), z_high),
    }
    line_devs = []
    for q in (3, 2, 1):
        other = (1 - z_low if q & 1 else z_low) + 2 * (1 - z_high if q & 2 else z_high)
        line_devs.append((other, (wide + 2 * (other - z_pos), narrow)))

    filled = [0, 0]
    flags = iter(range(g_recv.shape[0]))
    sent = []

    def remote(src, dst, dev, send_sem, recv_sem):
        pltpu.make_async_remote_copy(
            src_ref=src,
            dst_ref=dst,
            send_sem=send_sem,
            recv_sem=recv_sem,
            device_id=dev,
            device_id_type=MESH,
        ).start()

    def wait_for(ref, sem):
        pltpu.make_async_copy(ref, ref, sem).wait()

    def at(start, size):
        return pl.ds(pl.multiple_of(start, 8), size)

    def piece(k, base, size, kind, compute):
        starts, sizes, into = [base], [size], []
        for step in kind:
            place = z_pos if step == "z" else pairs[step][1]
            sizes.append(sizes[-1] // (4 if step == "z" else 2))
            starts.append(starts[-1] + place * sizes[-1])
        last = len(kind) - 1
        own = at(starts[-1], sizes[-1])
        flag = [g_recv.at[next(flags)] for _ in kind]
        back_flag = [g_recv.at[next(flags)]] + flag[:-1]
        out_flag = g_send.at[k]
        sent.append((k, 2 * (size - sizes[-1])))

        def scatter(i):
            part = sizes[i + 1]
            if kind[i] == "z":
                targets = line_devs
            else:
                dev, place = pairs[kind[i]]
                targets = [(1 - place, dev)]
            start = filled[k]
            into.append((start, part * len(targets)))
            filled[k] += part * len(targets)
            for q, (place, dev) in enumerate(targets):
                src = gp.at[k, at(starts[i] + place * part, part)]
                dst = arrived.at[k, pl.ds(start + q * part, part)]
                remote(src, dst, dev, out_flag, flag[i])

        def add(i):
            part = sizes[i + 1]
            start, total = into[i]
            wait_for(arrived.at[k, pl.ds(start, total)], flag[i])
            rows_here = at(starts[i + 1], part)
            value = gp[k, rows_here]
            for q in range(total // part):
                value = value + arrived[k, start + q * part : start + (q + 1) * part]
            return rows_here, value

        def gather(i):
            ref = g_full.at[k, at(starts[i + 1], sizes[i + 1])]
            targets = line_devs if kind[i] == "z" else [(0, pairs[kind[i]][0])]
            for _, dev in targets:
                remote(ref, ref, dev, out_flag, back_flag[i])

        def start():
            compute()
            scatter(0)

        def middle(i):
            rows_here, value = add(i)
            gp[k, rows_here] = value
            scatter(i + 1)

        def turn():
            _, value = add(last)
            for b in extra_bits:
                gp[k, own] = value
                into_more = arrived.at[k, pl.ds(filled[k], sizes[-1])]
                more = g_recv.at[next(flags)], g_recv.at[next(flags)]
                remote(gp.at[k, own], into_more, (flip(wide, b), narrow), *more)
                wait_for(into_more, more[0])
                wait_for(into_more, more[1])
                value = value + arrived[k, filled[k] : filled[k] + sizes[-1]]
                filled[k] += sizes[-1]
            g_full[k, own] = value * (1.0 / count)
            gather(last)

        def back(i):
            got = (3 if kind[i] == "z" else 1) * sizes[i + 1]
            wait_for(g_full.at[k, pl.ds(base, got)], back_flag[i])
            if i:
                gather(i - 1)

        return (
            [start]
            + [functools.partial(middle, i) for i in range(last)]
            + [turn]
            + [functools.partial(back, i) for i in range(last, -1, -1)]
        )

    def clear_ends(grid):
        empty = jnp.zeros((line, 3 * chan), BF16)
        grid[0:line, :] = empty
        grid[line + rows : 2 * line + rows, :] = empty

    clear_ends(x_one)
    got_mask.wait()
    hist = mk.shape[0]
    width = chan // hist
    spot = lax.broadcasted_iota(jnp.int32, (pos, line), 1)
    owner = SIDE * lax.broadcasted_iota(jnp.int32, (pos, line), 0)
    spread_pos = jnp.where((spot >= owner) & (spot < owner + SIDE), 1.0, 0.0).astype(BF16)
    spot = lax.broadcasted_iota(jnp.int32, (hist, chan), 1)
    owner = width * lax.broadcasted_iota(jnp.int32, (hist, chan), 0)
    spread_chan = jnp.where((spot >= owner) & (spot < owner + width), 1.0, 0.0).astype(BF16)
    by_row = dot(mk[...].astype(F32).astype(BF16), spread_pos, 1, 0).astype(BF16)
    planes = dot(by_row, spread_chan, 0, 0)

    pltpu.make_async_copy(bd, bd, load_sem.at[1]).wait()
    for i in range(SIDE):
        value = bd[i].reshape(line, chan) * planes
        bd[i] = value.reshape(pos, SIDE, chan)
        put_shifted(x_one, i, value)

    for a in range(3):
        got_k0[a].wait()
        part = slice(a * chunk, (a + 1) * chunk)
        wb[0, :, part] = kf[:, part].astype(BF16)
    conv(x_one, 0, h_one)
    local = local_moments(h_one)
    pl.semaphore_wait(barrier, nw * nn - 1)
    share(0, local)

    got_par.wait()

    def keep_share(k):
        share_width = kt.shape[1]
        span = -(-(share_width + 64) // 128) * 128
        start = narrow * share_width
        block = (start // 128) * 128
        d_hid[0:span, :] = kf[:, pl.ds(pl.multiple_of(block, 128), span)].T
        kt[k] = d_hid[pl.ds(pl.multiple_of(start - block, 8), share_width), :]

    clear_ends(x_two)
    clear_ends(dgrid)
    keep_share(0)
    got_k1 = load(4, kernels.at[1], kf)
    for i in range(SIDE):
        load(5, cotangent.at[:, i], ct.at[i])
    late = [
        load(6, momenta, mom),
        load(7, left_stats, lstats_v),
        load(8, left_roots, lroots_v),
        load(12, right_roots, roots_v),
        load(2, right_stats, stats_v),
    ]
    got_k1.wait()
    wb[1] = kf[...].astype(BF16)
    keep_share(1)

    gain_one, shift_one = par[0, 0:1, :], par[0, 1:2, :]
    gain_two, shift_two = par[1, 0:1, :], par[1, 1:2, :]

    mean_one, inv_one = moments(0)

    @pl.loop(0, SIDE)
    def _(i):
        at = at_line(i)
        normed = (h_one[at, :] - mean_one) * inv_one
        h_one[at, :] = normed
        pre = normed * gain_one + shift_one
        put_shifted(x_two, i, (0.5 * pre) * (1.0 + gelu_tanh(pre)))

    conv(x_two, 1, h_two)
    share(1, local_moments(h_two))

    @pl.loop(0, SIDE)
    def _(i):
        at = at_line(i)
        pre = h_one[at, :] * gain_one + shift_one
        slope_one[at, :] = gelu_slope(pre, gelu_tanh(pre))

    pltpu.make_async_copy(ct, ct, load_sem.at[5]).wait()
    mean_two, inv_two = moments(1)

    def fold(value):
        return jnp.sum(value.reshape(pos, SIDE, chan), axis=0)

    nothing = jnp.zeros((SIDE, chan), F32)

    def close(gain_sum, shift_sum):
        return jnp.concatenate(
            [
                jnp.sum(gain_sum, axis=0, keepdims=True),
                jnp.sum(shift_sum, axis=0, keepdims=True),
            ],
            axis=0,
        )

    def out_line(i, carry):
        at = at_line(i)
        normed = (h_two[at, :] - mean_two) * inv_two
        h_two[at, :] = normed
        summed = bd[i].reshape(line, chan) + normed * gain_two + shift_two
        t = gelu_tanh(summed)
        bo[i] = ((0.5 * summed) * (1.0 + t)).reshape(pos, SIDE, chan)
        slope = ct[i].reshape(line, chan) * gelu_slope(summed, t)
        d_sum[at, :] = slope
        return carry[0] + fold(slope * normed), carry[1] + fold(slope)

    share(2, close(*lax.fori_loop(0, SIDE, out_line, (nothing, nothing))))

    gain_two_sum, shift_two_sum = totals(2)
    scale_two = gain_two * inv_two

    @pl.loop(0, SIDE)
    def _(i):
        at = at_line(i)
        lost = (shift_two_sum + h_two[at, :] * gain_two_sum) * (1.0 / count)
        put_shifted(dgrid, i, scale_two * (d_sum[at, :] - lost))

    def weights(k, first, taps_here):
        grid = (x_one, x_two)[k]
        tap = first
        while tap < first + taps_here:
            a, b = divmod(tap, 3)
            n = min(3 - b, first + taps_here - tap)
            g_part = dot(
                grid[a * line : a * line + rows, b * chan : (b + n) * chan],
                dgrid[line : line + rows, chan : 2 * chan],
                0,
                0,
            )
            gp[k, tap * chan : (tap + n) * chan, :] = g_part
            tap += n

    def add_back(k, a):
        term = conv_back(dgrid, k, a)
        d_hid[...] = d_hid[...] + term if a else term

    kept = {}

    def pre_sums():
        def pre_line(i, carry):
            at = at_line(i)
            d_pre = d_hid[at, :] * slope_one[at, :]
            d_hid[at, :] = d_pre
            return carry[0] + fold(d_pre * h_one[at, :]), carry[1] + fold(d_pre)

        share(3, close(*lax.fori_loop(0, SIDE, pre_line, (nothing, nothing))))

    def first_conv_grad():
        kept["sums"] = gain_one_sum, shift_one_sum = totals(3)
        scale_one = gain_one * inv_one

        @pl.loop(0, SIDE)
        def _(i):
            at = at_line(i)
            lost = (shift_one_sum + h_one[at, :] * gain_one_sum) * (1.0 / count)
            put_shifted(dgrid, i, scale_one * (d_hid[at, :] - lost))

    def board_grads():
        for i in range(SIDE):
            at = at_line(i)
            bg[i] = ((d_sum[at, :] + d_hid[at, :]) * planes).reshape(pos, SIDE, chan)

    def second_left():
        for copy in late:
            copy.wait()
        for a in range(3):
            x_two[0:chunk, a * chan : (a + 1) * chan] = g_full[
                1, a * chunk : (a + 1) * chunk, :
            ].astype(BF16)
        blocks = [x_two[0:chunk, a * chan : (a + 1) * chan] for a in range(3)]
        term = sum(dot(block, block, 0, 0) for block in blocks)
        lstats_v[1] = STAT_DECAY * lstats_v[1] + (1.0 - STAT_DECAY) * term

    def second_right(a):
        width = kt.shape[1]
        start = pl.multiple_of(narrow * width, 8)
        own = g_full[1, pl.ds(start, width), :].astype(BF16)
        cols = slice(a * chunk, (a + 1) * chunk)
        term = dot(own, x_two[0:chunk, a * chan : (a + 1) * chan], 1, 1)
        stats_v[1, :, cols] = STAT_DECAY * stats_v[1, :, cols] + (1.0 - STAT_DECAY) * term

    def second_kernel():
        mixed = sum(
            dot(
                roots_v[1, :, a * chunk : (a + 1) * chunk].astype(BF16),
                x_two[0:chunk, a * chan : (a + 1) * chan],
                1,
                0,
            )
            for a in range(3)
        )
        update = dot(mixed.astype(BF16), lroots_v[1].astype(BF16), 1, 1)
        kt[1] = kt[1] - KERNEL_RATE * update

    steps = []
    tap_at = [0, 0]
    for k, n, kind in PIECES:
        compute = functools.partial(weights, k, tap_at[k], n)
        steps.append(iter(piece(k, tap_at[k] * chan, n * chan, kind, compute)))
        tap_at[k] += n
    passes = {
        -1: iter([functools.partial(add_back, 1, a) for a in range(3)]),
        -2: iter([pre_sums]),
        -3: iter([first_conv_grad]),
        -4: iter([functools.partial(add_back, 0, a) for a in range(3)]),
        -5: iter([board_grads]),
        -7: iter([second_left, lambda: (second_right(0), second_right(1)), lambda: second_right(2), second_kernel]),
    }
    for item in ORDER:
        next(steps[item] if item >= 0 else passes[item])()
    gain_one_sum, shift_one_sum = kept["sums"]

    norm_grad = [
        jnp.concatenate([gain_one_sum, shift_one_sum], axis=0),
        jnp.concatenate([gain_two_sum, shift_two_sum], axis=0),
    ]
    for k in range(2):
        value = MOMENTUM * mom[k] + norm_grad[k] * (1.0 / count)
        new_momenta[k] = value
        new_params[k] = par[k] - NORM_RATE * value

    sent_all(3)
    for k in range(2):
        size = sum(part for layer, part in sent if layer == k)
        wait_for(stats_v.at[k, pl.ds(0, size * chan // kin)], g_send.at[k])


def finish_kernel(
    dims,
    g_full,
    stats,
    roots,
    lstats,
    lroots,
    kt,
    bo,
    bg,
    momenta,
    params,
    o_block,
    o_board,
    o_grad,
    o_kernel,
    o_left,
    o_right,
    o_momenta,
    o_params,
    gb,
    nr,
    nk,
    nl,
    sem,
):
    chan = dims[3]
    chunk = 3 * chan
    share_width = kt.shape[1]
    start = pl.multiple_of(lax.axis_index("narrow") * share_width, 8)

    def put(slot, src, dst):
        pltpu.make_async_copy(src, dst, sem.at[slot]).start()

    put(0, stats.at[1], o_right.at[1])
    for k in range(2):
        put(1, g_full.at[k, pl.ds(start, share_width)], o_grad.at[k])
    put(2, kt.at[1], o_kernel.at[1])
    put(3, lstats.at[1], o_left.at[1])
    for i in range(SIDE):
        put(4, bo.at[i], o_block.at[:, i])
        put(5, bg.at[i], o_board.at[:, i])
    put(6, momenta, o_momenta)
    put(7, params, o_params)
    gb[...] = g_full[0].astype(BF16)
    own = g_full[0, pl.ds(start, share_width), :].astype(BF16)
    for q in range(3):
        cols = pl.ds(q * chunk, chunk)
        term = dot(own, gb[cols, :], 1, 1)
        nr[q] = STAT_DECAY * stats[0, :, cols] + (1.0 - STAT_DECAY) * term
        put(8, nr.at[q], o_right.at[0, :, cols])
    term = dot(gb[...], gb[...], 0, 0)
    nl[...] = STAT_DECAY * lstats[0] + (1.0 - STAT_DECAY) * term
    put(9, nl, o_left.at[0])
    mixed = dot(roots[0].astype(BF16), gb[...], 1, 0)
    update = dot(mixed.astype(BF16), lroots[0].astype(BF16), 1, 1)
    nk[...] = kt[0] - KERNEL_RATE * update
    put(10, nk, o_kernel.at[0])
    wholes = (stats.at[1], kt, nk, nl, bo, bg, momenta, params, nr, nl, nk)
    for slot, whole in enumerate(wholes):
        pltpu.make_async_copy(whole, whole, sem.at[slot]).wait()


def room_of(size, kind, extra):
    rows = 0
    for step in kind:
        size //= 4 if step == "z" else 2
        rows += 3 * size if step == "z" else size
    return rows + extra * size


def body(
    nw,
    nn,
    boards,
    history_mask,
    kernels,
    norm_params,
    norm_momenta,
    left_stats,
    right_stats,
    left_roots,
    right_roots,
    out_cotangent,
):
    pos, chan = boards.shape[0], boards.shape[3]
    kin = kernels.shape[2]
    share_width = right_stats.shape[2]
    line = pos * SIDE
    rows = line * SIDE
    chunk = 3 * chan
    ndev = nw * nn
    extra = max(nw.bit_length() - 4, 0)
    dims = (nw, nn, pos, chan)
    hbm = pl.BlockSpec(memory_space=pl.ANY)
    vmem = pl.BlockSpec(memory_space=pltpu.VMEM)
    board_shape = (SIDE, pos, SIDE, chan)

    kept = [
        (2, kin, chan),
        (2, share_width, kin),
        (2, share_width, kin),
        (2, chan, chan),
        (2, chan, chan),
        (2, share_width, chan),
        board_shape,
        board_shape,
        (2, 2, chan),
        (2, 2, chan),
    ]
    arrivals = max(
        sum(room_of(n * chan, kind, extra) for layer, n, kind in PIECES if layer == k)
        for k in range(2)
    )
    flags = sum(len(kind) + 1 + 2 * extra for _, _, kind in PIECES)
    room = (49 + extra) * MIB // 2 + (ndev - 32) * 8 * chan * 4 + 8 * chan * max(arrivals - kin, 0)
    fused = pl.pallas_call(
        functools.partial(fused_kernel, dims),
        out_shape=[pltpu.VMEM(shape, F32) for shape in kept],
        in_specs=[hbm] * 10,
        out_specs=[vmem] * len(kept),
        scratch_shapes=[
            pltpu.VMEM(board_shape, F32),
            pltpu.VMEM(board_shape, F32),
            pltpu.VMEM(history_mask.shape[::-1], jnp.int32),
            pltpu.VMEM((2, 2, chan), F32),
            pltpu.VMEM((2, 2, chan), F32),
            pltpu.VMEM((chan, kin), F32),
            pltpu.VMEM((2, chan, kin), BF16),
            pltpu.VMEM((rows + 2 * line, chunk), BF16),
            pltpu.VMEM((rows + 2 * line, chunk), BF16),
            pltpu.VMEM((rows + 2 * line, chunk), BF16),
            pltpu.VMEM((rows, chan), F32),
            pltpu.VMEM((rows, chan), F32),
            pltpu.VMEM((rows, chan), F32),
            pltpu.VMEM((rows, chan), F32),
            pltpu.VMEM((rows, chan), F32),
            pltpu.VMEM((2, kin, chan), F32),
            pltpu.VMEM((4, ndev, 2, chan), F32),
            pltpu.VMEM((2, arrivals, chan), F32),
            pltpu.SemaphoreType.DMA((13,)),
            pltpu.SemaphoreType.DMA((1,)),
            pltpu.SemaphoreType.DMA((2,)),
            pltpu.SemaphoreType.DMA((2,)),
            pltpu.SemaphoreType.DMA((flags,)),
        ],
        compiler_params=pltpu.CompilerParams(
            collective_id=0, has_side_effects=True, vmem_limit_bytes=room
        ),
        name="fused_passes",
    )
    given = (
        boards,
        history_mask.T,
        kernels,
        norm_params,
        norm_momenta,
        left_stats,
        left_roots,
        jnp.swapaxes(right_stats, 1, 2),
        jnp.swapaxes(right_roots, 1, 2),
        out_cotangent,
    )
    held = fused(*(pltpu.with_memory_space_constraint(v, pltpu.HBM) for v in given))
    held = [pltpu.with_memory_space_constraint(v, pltpu.VMEM) for v in held]
    finish = pl.pallas_call(
        functools.partial(finish_kernel, dims),
        out_shape=[
            pltpu.HBM(boards.shape, F32),
            pltpu.HBM(boards.shape, F32),
            pltpu.HBM((2, share_width, chan), F32),
            pltpu.HBM((2, share_width, chan), F32),
            pltpu.HBM((2, chan, chan), F32),
            pltpu.HBM((2, share_width, kin), F32),
            pltpu.HBM((2, 2, chan), F32),
            pltpu.HBM((2, 2, chan), F32),
        ],
        in_specs=[vmem] * len(kept),
        out_specs=[hbm] * 8,
        scratch_shapes=[
            pltpu.VMEM((kin, chan), BF16),
            pltpu.VMEM((3, share_width, chunk), F32),
            pltpu.VMEM((share_width, chan), F32),
            pltpu.VMEM((chan, chan), F32),
            pltpu.SemaphoreType.DMA((11,)),
        ],
        compiler_params=pltpu.CompilerParams(vmem_limit_bytes=20 * MIB),
        name="finish",
    )
    block_out, board_grad, grad, kernel, left, right, momenta, params = finish(*held)
    return (
        block_out,
        board_grad,
        jnp.swapaxes(grad, 1, 2),
        jnp.swapaxes(kernel, 1, 2),
        left,
        jnp.swapaxes(right, 1, 2),
        momenta,
        params,
    )


def solution(mesh):
    nw, nn = mesh.shape["wide"], mesh.shape["narrow"]
    boards = P(("wide", "narrow"), None, None, None)
    columns = P(None, None, "narrow")
    in_specs = (
        boards,
        P(("wide", "narrow"), None),
        P(),
        P(),
        P(),
        P(),
        columns,
        P(),
        columns,
        boards,
    )
    out_specs = (boards, boards, columns, columns, P(), columns, P(), P())
    return jax.shard_map(
        functools.partial(body, nw, nn),
        mesh=mesh,
        in_specs=in_specs,
        out_specs=out_specs,
        check_vma=False,
    )
```

```python
import functools
import math

import jax
import jax.numpy as jnp
from jax import lax
from jax.experimental import pallas as pl
from jax.experimental.pallas import tpu as pltpu
from jax.sharding import PartitionSpec as P

EPS = 1e-05
MOMENTUM = 0.9
NORM_RATE = 50.0
KERNEL_RATE = 0.1
STAT_DECAY = 0.5

SIDE = 8
CUBE = 0.044715
ROOT = math.sqrt(2.0 / math.pi)
MESH = pl.DeviceIdType.MESH
F32 = jnp.float32
BF16 = jnp.bfloat16
MIB = 2**20


PIECES = (
    (1, 1, "cab12"), (1, 1, "c12ab"), (1, 1, "c12z"), (1, 1, "cz12"),
    (1, 1, "c12ab"), (1, 1, "c12ab"), (1, 1, "c12z"), (1, 1, "c12z"),
    (1, 1, "c12z"), (0, 1, "c12ab"), (0, 1, "cz12"), (0, 1, "c12z"),
    (0, 1, "c12z"), (0, 1, "c12z"), (0, 1, "c12ab"), (0, 1, "c12z"),
    (0, 1, "c12z"), (0, 1, "c12ab"),
)
ORDER = (
    5, -1, 0, 1, -1, 5, 4, -1, -2, 1, 0, 7, 3, 4, 2, 6, 7, 3, 2, 8,
    6, 5, 8, 1, 0, -3, 10, 17, 12, 4, 7, 14, 15, 5, 2, 10, 17, 16, 9, 14,
    6, 1, 12, 13, 4, 11, 8, 7, 9, 5, 0, 2, 15, 17, 6, -4, 13, 16, 1, 14,
    4, 12, 8, 5, 9, 7, 3, 0, 17, 2, 15, 10, 11, 14, 6, -4, 4, 13, 1, 12,
    9, 8, 0, 5, 16, 3, 7, 15, 14, 10, 17, 11, 2, 13, 4, 9, 6, 1, 16, 3,
    0, 5, 12, 7, 8, 11, 10, 2, 14, 15, 17, 4, 1, 9, 3, 13, 5, 6, 16, 8,
    12, 0, 14, 10, 11, 1, 17, 2, 15, 9, 4, 3, 13, 6, 12, 16, 5, 14, -4, 0,
    17, 1, 15, 8, 11, 10, 13, 4, 9, 7, 16, 14, 4, 5, 2, 17, 3, 8, 11, 7,
    0, 15, 6, 9, 12, 1, 13, 3, 16, 0, -7, 14, 12, -7, -7, 13, 17, 11, 10, 15,
    16, 14, 9, -7, -5, 17, 11, 10, 9,
)


def dot(lhs, rhs, lhs_dim, rhs_dim):
    return lax.dot_general(
        lhs, rhs, (((lhs_dim,), (rhs_dim,)), ((), ())), preferred_element_type=F32
    )


def gelu_tanh(v):
    return jnp.tanh(ROOT * (v + CUBE * (v * v * v)))


def gelu_slope(v, t):
    inner = ROOT * (1.0 + (3.0 * CUBE) * (v * v))
    return 0.5 * (1.0 + t) + (0.5 * v) * ((1.0 - t * t) * inner)


def flip(index, bit):
    return index + (1 - 2 * ((index // (1 << bit)) % 2)) * (1 << bit)


def bit_of(index, bit):
    return (index // (1 << bit)) % 2


def pick(taken, one, other):
    return taken * one + (1 - taken) * other


def fused_kernel(
    dims,
    boards,
    mask_t,
    kernels,
    params,
    momenta,
    left_stats,
    left_roots,
    right_stats,
    right_roots,
    cotangent,
    g_full,
    stats_v,
    roots_v,
    lstats_v,
    lroots_v,
    kt,
    bo,
    bg,
    new_momenta,
    new_params,
    bd,
    ct,
    mk,
    par,
    mom,
    kf,
    wb,
    x_one,
    x_two,
    dgrid,
    h_one,
    slope_one,
    h_two,
    d_sum,
    d_hid,
    gp,
    red,
    arrived,
    load_sem,
    red_send,
    red_recv,
    g_send,
    g_recv,
):
    nw, nn, pos, chan = dims
    line = pos * SIDE
    rows = line * SIDE
    count = float(rows * nw * nn)
    chunk = 3 * chan
    kin = 9 * chan
    wide, narrow = lax.axis_index("wide"), lax.axis_index("narrow")
    me = wide * nn + narrow
    extra_bits = list(range(3, nw.bit_length() - 1))

    def load(slot, src, dst):
        copy = pltpu.make_async_copy(src, dst, load_sem.at[slot])
        copy.start()
        return copy

    got_mask = load(0, mask_t, mk)
    for i in range(SIDE):
        load(1, boards.at[:, i], bd.at[i])
    got_k0 = [
        load(9 + a, kernels.at[0, :, pl.ds(a * chunk, chunk)], kf.at[:, pl.ds(a * chunk, chunk)])
        for a in range(3)
    ]
    got_par = load(3, params, par)

    def each_other(act):
        if nw * nn <= 32:
            for k in range(nw * nn - 1, 0, -1):
                w, n = wide, narrow
                for b in range(nw.bit_length() - 1):
                    if (k // nn) >> b & 1:
                        w = flip(w, b) if b == 0 else w + (flip(wide, b) - wide)
                for b in range(nn.bit_length() - 1):
                    if (k % nn) >> b & 1:
                        n = n + (flip(narrow, b) - narrow)
                act((w, n))
        else:

            @pl.loop(1, nw * nn)
            def _(k):
                other = lax.rem(me + k, nw * nn)
                act((other // nn, lax.rem(other, nn)))

    barrier = pltpu.get_barrier_semaphore()
    each_other(
        lambda dev: pl.semaphore_signal(barrier, inc=1, device_id=dev, device_id_type=MESH)
    )

    def share(slot, value):
        red[slot, me] = value
        if slot:
            sent_all(slot - 1)

        def send(dev):
            pltpu.make_async_remote_copy(
                src_ref=red.at[slot, me],
                dst_ref=red.at[slot, me],
                send_sem=red_send.at[0],
                recv_sem=red_recv.at[slot % 2],
                device_id=dev,
                device_id_type=MESH,
            ).start()

        each_other(send)

    def collect(slot):
        others = red.at[slot, pl.ds(0, nw * nn - 1)]
        pltpu.make_async_copy(others, others, red_recv.at[slot % 2]).wait()
        return red[slot]

    def sent_all(slot):
        others = red.at[slot, pl.ds(0, nw * nn - 1)]
        pltpu.make_async_copy(others, others, red_send.at[0]).wait()

    def moments(slot):
        got = collect(slot)
        means, spreads = got[:, 0, :], got[:, 1, :]
        mean = jnp.sum(means, axis=0, keepdims=True) * (1.0 / (nw * nn))
        gap = means - mean
        spread = jnp.sum(spreads, axis=0, keepdims=True) + float(rows) * jnp.sum(
            gap * gap, axis=0, keepdims=True
        )
        return mean, lax.rsqrt(spread / count + EPS)

    def totals(slot):
        got = collect(slot)
        return (
            jnp.sum(got[:, 0, :], axis=0, keepdims=True),
            jnp.sum(got[:, 1, :], axis=0, keepdims=True),
        )

    def local_moments(ref):
        total = jnp.sum(ref[...], axis=0, keepdims=True)
        mean = total * (1.0 / rows)
        gap = ref[...] - mean
        return jnp.concatenate([mean, jnp.sum(gap * gap, axis=0, keepdims=True)], axis=0)

    column = lax.broadcasted_iota(jnp.int32, (pos, SIDE, chan), 1)

    def put_shifted(grid, i, value):
        cube = value.reshape(pos, SIDE, chan)
        before = jnp.where(column == 0, 0.0, pltpu.roll(cube, 1, 1))
        after = jnp.where(column == SIDE - 1, 0.0, pltpu.roll(cube, SIDE - 1, 1))
        at = pl.ds(pl.multiple_of((i + 1) * line, 16), line)
        grid[at, 0:chan] = before.reshape(line, chan).astype(BF16)
        grid[at, chan : 2 * chan] = value.astype(BF16)
        grid[at, 2 * chan : 3 * chan] = after.reshape(line, chan).astype(BF16)

    def at_line(i):
        return pl.ds(pl.multiple_of(i * line, 8), line)

    def conv(grid, k, result):
        tile = rows // 2

        @pl.loop(0, 2)
        def _(i):
            result[pl.ds(pl.multiple_of(i * tile, 8), tile), :] = sum(
                dot(
                    grid[pl.ds(pl.multiple_of(a * line + i * tile, 16), tile), :],
                    wb[k, :, a * chunk : (a + 1) * chunk],
                    1,
                    1,
                )
                for a in range(3)
            )

    def conv_back(grid, k, a):
        result = None
        for b in range(3):
            tap = 3 * (2 - a) + (2 - b)
            term = dot(
                grid[a * line : a * line + rows, b * chan : (b + 1) * chan],
                wb[k, :, tap * chan : (tap + 1) * chan],
                1,
                0,
            )
            result = term if result is None else result + term
        return result

    core = bit_of(narrow, 0)
    x_bit, y_bit = bit_of(narrow, 1), bit_of(wide, 0)
    z_low, z_high = bit_of(wide, 1), bit_of(wide, 2)
    z_pos = z_low + 2 * z_high
    x_dev = (wide, flip(narrow, 1))
    y_dev = (flip(wide, 0), narrow)
    pairs = {
        "c": ((wide, flip(narrow, 0)), core),
        "1": (
            (pick(core, y_dev[0], x_dev[0]), pick(core, y_dev[1], x_dev[1])),
            pick(core, y_bit, x_bit),
        ),
        "2": (
            (pick(core, x_dev[0], y_dev[0]), pick(core, x_dev[1], y_dev[1])),
            pick(core, x_bit, y_bit),
        ),
        "a": ((flip(wide, 1), narrow), z_low),
        "b": ((flip(wide, 2), narrow), z_high),
    }
    line_devs = []
    for q in (3, 2, 1):
        other = (1 - z_low if q & 1 else z_low) + 2 * (1 - z_high if q & 2 else z_high)
        line_devs.append((other, (wide + 2 * (other - z_pos), narrow)))

    filled = [0, 0]
    flags = iter(range(g_recv.shape[0]))
    sent = []

    def remote(src, dst, dev, send_sem, recv_sem):
        pltpu.make_async_remote_copy(
            src_ref=src,
            dst_ref=dst,
            send_sem=send_sem,
            recv_sem=recv_sem,
            device_id=dev,
            device_id_type=MESH,
        ).start()

    def wait_for(ref, sem):
        pltpu.make_async_copy(ref, ref, sem).wait()

    def at(start, size):
        return pl.ds(pl.multiple_of(start, 8), size)

    def piece(k, base, size, kind, compute):
        starts, sizes, into = [base], [size], []
        for step in kind:
            place = z_pos if step == "z" else pairs[step][1]
            sizes.append(sizes[-1] // (4 if step == "z" else 2))
            starts.append(starts[-1] + place * sizes[-1])
        last = len(kind) - 1
        own = at(starts[-1], sizes[-1])
        flag = [g_recv.at[next(flags)] for _ in kind]
        back_flag = [g_recv.at[next(flags)]] + flag[:-1]
        out_flag = g_send.at[k]
        sent.append((k, 2 * (size - sizes[-1])))

        def scatter(i):
            part = sizes[i + 1]
            if kind[i] == "z":
                targets = line_devs
            else:
                dev, place = pairs[kind[i]]
                targets = [(1 - place, dev)]
            start = filled[k]
            into.append((start, part * len(targets)))
            filled[k] += part * len(targets)
            for q, (place, dev) in enumerate(targets):
                src = gp.at[k, at(starts[i] + place * part, part)]
                dst = arrived.at[k, pl.ds(start + q * part, part)]
                remote(src, dst, dev, out_flag, flag[i])

        def add(i):
            part = sizes[i + 1]
            start, total = into[i]
            wait_for(arrived.at[k, pl.ds(start, total)], flag[i])
            rows_here = at(starts[i + 1], part)
            value = gp[k, rows_here]
            for q in range(total // part):
                value = value + arrived[k, start + q * part : start + (q + 1) * part]
            return rows_here, value

        def gather(i):
            ref = g_full.at[k, at(starts[i + 1], sizes[i + 1])]
            targets = line_devs if kind[i] == "z" else [(0, pairs[kind[i]][0])]
            for _, dev in targets:
                remote(ref, ref, dev, out_flag, back_flag[i])

        def start():
            compute()
            scatter(0)

        def middle(i):
            rows_here, value = add(i)
            gp[k, rows_here] = value
            scatter(i + 1)

        def turn():
            _, value = add(last)
            for b in extra_bits:
                gp[k, own] = value
                into_more = arrived.at[k, pl.ds(filled[k], sizes[-1])]
                more = g_recv.at[next(flags)], g_recv.at[next(flags)]
                remote(gp.at[k, own], into_more, (flip(wide, b), narrow), *more)
                wait_for(into_more, more[0])
                wait_for(into_more, more[1])
                value = value + arrived[k, filled[k] : filled[k] + sizes[-1]]
                filled[k] += sizes[-1]
            g_full[k, own] = value * (1.0 / count)
            gather(last)

        def back(i):
            got = (3 if kind[i] == "z" else 1) * sizes[i + 1]
            wait_for(g_full.at[k, pl.ds(base, got)], back_flag[i])
            if i:
                gather(i - 1)

        return (
            [start]
            + [functools.partial(middle, i) for i in range(last)]
            + [turn]
            + [functools.partial(back, i) for i in range(last, -1, -1)]
        )

    def clear_ends(grid):
        empty = jnp.zeros((line, 3 * chan), BF16)
        grid[0:line, :] = empty
        grid[line + rows : 2 * line + rows, :] = empty

    clear_ends(x_one)
    got_mask.wait()
    hist = mk.shape[0]
    width = chan // hist
    spot = lax.broadcasted_iota(jnp.int32, (pos, line), 1)
    owner = SIDE * lax.broadcasted_iota(jnp.int32, (pos, line), 0)
    spread_pos = jnp.where((spot >= owner) & (spot < owner + SIDE), 1.0, 0.0).astype(BF16)
    spot = lax.broadcasted_iota(jnp.int32, (hist, chan), 1)
    owner = width * lax.broadcasted_iota(jnp.int32, (hist, chan), 0)
    spread_chan = jnp.where((spot >= owner) & (spot < owner + width), 1.0, 0.0).astype(BF16)
    by_row = dot(mk[...].astype(F32).astype(BF16), spread_pos, 1, 0).astype(BF16)
    planes = dot(by_row, spread_chan, 0, 0)

    pltpu.make_async_copy(bd, bd, load_sem.at[1]).wait()
    for i in range(SIDE):
        value = bd[i].reshape(line, chan) * planes
        bd[i] = value.reshape(pos, SIDE, chan)
        put_shifted(x_one, i, value)

    for a in range(3):
        got_k0[a].wait()
        part = slice(a * chunk, (a + 1) * chunk)
        wb[0, :, part] = kf[:, part].astype(BF16)
    conv(x_one, 0, h_one)
    local = local_moments(h_one)
    pl.semaphore_wait(barrier, nw * nn - 1)
    share(0, local)

    got_par.wait()

    def keep_share(k):
        share_width = kt.shape[1]
        span = -(-(share_width + 64) // 128) * 128
        start = narrow * share_width
        block = (start // 128) * 128
        d_hid[0:span, :] = kf[:, pl.ds(pl.multiple_of(block, 128), span)].T
        kt[k] = d_hid[pl.ds(pl.multiple_of(start - block, 8), share_width), :]

    clear_ends(x_two)
    clear_ends(dgrid)
    keep_share(0)
    got_k1 = load(4, kernels.at[1], kf)
    for i in range(SIDE):
        load(5, cotangent.at[:, i], ct.at[i])
    late = [
        load(6, momenta, mom),
        load(7, left_stats, lstats_v),
        load(8, left_roots, lroots_v),
        load(12, right_roots, roots_v),
        load(2, right_stats, stats_v),
    ]
    got_k1.wait()
    wb[1] = kf[...].astype(BF16)
    keep_share(1)

    gain_one, shift_one = par[0, 0:1, :], par[0, 1:2, :]
    gain_two, shift_two = par[1, 0:1, :], par[1, 1:2, :]

    mean_one, inv_one = moments(0)

    @pl.loop(0, SIDE)
    def _(i):
        at = at_line(i)
        normed = (h_one[at, :] - mean_one) * inv_one
        h_one[at, :] = normed
        pre = normed * gain_one + shift_one
        put_shifted(x_two, i, (0.5 * pre) * (1.0 + gelu_tanh(pre)))

    conv(x_two, 1, h_two)
    share(1, local_moments(h_two))

    @pl.loop(0, SIDE)
    def _(i):
        at = at_line(i)
        pre = h_one[at, :] * gain_one + shift_one
        slope_one[at, :] = gelu_slope(pre, gelu_tanh(pre))

    pltpu.make_async_copy(ct, ct, load_sem.at[5]).wait()
    mean_two, inv_two = moments(1)

    def fold(value):
        return jnp.sum(value.reshape(pos, SIDE, chan), axis=0)

    nothing = jnp.zeros((SIDE, chan), F32)

    def close(gain_sum, shift_sum):
        return jnp.concatenate(
            [
                jnp.sum(gain_sum, axis=0, keepdims=True),
                jnp.sum(shift_sum, axis=0, keepdims=True),
            ],
            axis=0,
        )

    def out_line(i, carry):
        at = at_line(i)
        normed = (h_two[at, :] - mean_two) * inv_two
        h_two[at, :] = normed
        summed = bd[i].reshape(line, chan) + normed * gain_two + shift_two
        t = gelu_tanh(summed)
        bo[i] = ((0.5 * summed) * (1.0 + t)).reshape(pos, SIDE, chan)
        slope = ct[i].reshape(line, chan) * gelu_slope(summed, t)
        d_sum[at, :] = slope
        return carry[0] + fold(slope * normed), carry[1] + fold(slope)

    share(2, close(*lax.fori_loop(0, SIDE, out_line, (nothing, nothing))))

    gain_two_sum, shift_two_sum = totals(2)
    scale_two = gain_two * inv_two

    @pl.loop(0, SIDE)
    def _(i):
        at = at_line(i)
        lost = (shift_two_sum + h_two[at, :] * gain_two_sum) * (1.0 / count)
        put_shifted(dgrid, i, scale_two * (d_sum[at, :] - lost))

    def weights(k, first, taps_here):
        grid = (x_one, x_two)[k]
        tap = first
        while tap < first + taps_here:
            a, b = divmod(tap, 3)
            n = min(3 - b, first + taps_here - tap)
            g_part = dot(
                grid[a * line : a * line + rows, b * chan : (b + n) * chan],
                dgrid[line : line + rows, chan : 2 * chan],
                0,
                0,
            )
            gp[k, tap * chan : (tap + n) * chan, :] = g_part
            tap += n

    def add_back(k, a):
        term = conv_back(dgrid, k, a)
        d_hid[...] = d_hid[...] + term if a else term

    kept = {}

    def pre_sums():
        def pre_line(i, carry):
            at = at_line(i)
            d_pre = d_hid[at, :] * slope_one[at, :]
            d_hid[at, :] = d_pre
            return carry[0] + fold(d_pre * h_one[at, :]), carry[1] + fold(d_pre)

        share(3, close(*lax.fori_loop(0, SIDE, pre_line, (nothing, nothing))))

    def first_conv_grad():
        kept["sums"] = gain_one_sum, shift_one_sum = totals(3)
        scale_one = gain_one * inv_one

        @pl.loop(0, SIDE)
        def _(i):
            at = at_line(i)
            lost = (shift_one_sum + h_one[at, :] * gain_one_sum) * (1.0 / count)
            put_shifted(dgrid, i, scale_one * (d_hid[at, :] - lost))

    def board_grads():
        for i in range(SIDE):
            at = at_line(i)
            bg[i] = ((d_sum[at, :] + d_hid[at, :]) * planes).reshape(pos, SIDE, chan)

    def second_left():
        for copy in late:
            copy.wait()
        for a in range(3):
            x_two[0:chunk, a * chan : (a + 1) * chan] = g_full[
                1, a * chunk : (a + 1) * chunk, :
            ].astype(BF16)
        blocks = [x_two[0:chunk, a * chan : (a + 1) * chan] for a in range(3)]
        term = sum(dot(block, block, 0, 0) for block in blocks)
        lstats_v[1] = STAT_DECAY * lstats_v[1] + (1.0 - STAT_DECAY) * term

    def second_right(a):
        width = kt.shape[1]
        start = pl.multiple_of(narrow * width, 8)
        own = g_full[1, pl.ds(start, width), :].astype(BF16)
        cols = slice(a * chunk, (a + 1) * chunk)
        term = dot(own, x_two[0:chunk, a * chan : (a + 1) * chan], 1, 1)
        stats_v[1, :, cols] = STAT_DECAY * stats_v[1, :, cols] + (1.0 - STAT_DECAY) * term

    def second_kernel():
        mixed = sum(
            dot(
                roots_v[1, :, a * chunk : (a + 1) * chunk].astype(BF16),
                x_two[0:chunk, a * chan : (a + 1) * chan],
                1,
                0,
            )
            for a in range(3)
        )
        update = dot(mixed.astype(BF16), lroots_v[1].astype(BF16), 1, 1)
        kt[1] = kt[1] - KERNEL_RATE * update

    steps = []
    tap_at = [0, 0]
    for k, n, kind in PIECES:
        compute = functools.partial(weights, k, tap_at[k], n)
        steps.append(iter(piece(k, tap_at[k] * chan, n * chan, kind, compute)))
        tap_at[k] += n
    passes = {
        -1: iter([functools.partial(add_back, 1, a) for a in range(3)]),
        -2: iter([pre_sums]),
        -3: iter([first_conv_grad]),
        -4: iter([functools.partial(add_back, 0, a) for a in range(3)]),
        -5: iter([board_grads]),
        -7: iter([second_left, lambda: (second_right(0), second_right(1)), lambda: second_right(2), second_kernel]),
    }
    for item in ORDER:
        next(steps[item] if item >= 0 else passes[item])()
    gain_one_sum, shift_one_sum = kept["sums"]

    norm_grad = [
        jnp.concatenate([gain_one_sum, shift_one_sum], axis=0),
        jnp.concatenate([gain_two_sum, shift_two_sum], axis=0),
    ]
    for k in range(2):
        value = MOMENTUM * mom[k] + norm_grad[k] * (1.0 / count)
        new_momenta[k] = value
        new_params[k] = par[k] - NORM_RATE * value

    sent_all(3)
    for k in range(2):
        size = sum(part for layer, part in sent if layer == k)
        wait_for(stats_v.at[k, pl.ds(0, size * chan // kin)], g_send.at[k])


def finish_kernel(
    dims,
    g_full,
    stats,
    roots,
    lstats,
    lroots,
    kt,
    bo,
    bg,
    momenta,
    params,
    o_block,
    o_board,
    o_grad,
    o_kernel,
    o_left,
    o_right,
    o_momenta,
    o_params,
    gb,
    nr,
    nk,
    nl,
    sem,
):
    chan = dims[3]
    chunk = 3 * chan
    share_width = kt.shape[1]
    start = pl.multiple_of(lax.axis_index("narrow") * share_width, 8)

    def put(slot, src, dst):
        pltpu.make_async_copy(src, dst, sem.at[slot]).start()

    put(0, stats.at[1], o_right.at[1])
    for k in range(2):
        put(1, g_full.at[k, pl.ds(start, share_width)], o_grad.at[k])
    put(2, kt.at[1], o_kernel.at[1])
    put(3, lstats.at[1], o_left.at[1])
    for i in range(SIDE):
        put(4, bo.at[i], o_block.at[:, i])
        put(5, bg.at[i], o_board.at[:, i])
    put(6, momenta, o_momenta)
    put(7, params, o_params)
    gb[...] = g_full[0].astype(BF16)
    own = g_full[0, pl.ds(start, share_width), :].astype(BF16)
    for q in range(3):
        cols = pl.ds(q * chunk, chunk)
        term = dot(own, gb[cols, :], 1, 1)
        nr[q] = STAT_DECAY * stats[0, :, cols] + (1.0 - STAT_DECAY) * term
        put(8, nr.at[q], o_right.at[0, :, cols])
    term = dot(gb[...], gb[...], 0, 0)
    nl[...] = STAT_DECAY * lstats[0] + (1.0 - STAT_DECAY) * term
    put(9, nl, o_left.at[0])
    mixed = dot(roots[0].astype(BF16), gb[...], 1, 0)
    update = dot(mixed.astype(BF16), lroots[0].astype(BF16), 1, 1)
    nk[...] = kt[0] - KERNEL_RATE * update
    put(10, nk, o_kernel.at[0])
    wholes = (stats.at[1], kt, nk, nl, bo, bg, momenta, params, nr, nl, nk)
    for slot, whole in enumerate(wholes):
        pltpu.make_async_copy(whole, whole, sem.at[slot]).wait()


def room_of(size, kind, extra):
    rows = 0
    for step in kind:
        size //= 4 if step == "z" else 2
        rows += 3 * size if step == "z" else size
    return rows + extra * size


def body(
    nw,
    nn,
    boards,
    history_mask,
    kernels,
    norm_params,
    norm_momenta,
    left_stats,
    right_stats,
    left_roots,
    right_roots,
    out_cotangent,
):
    pos, chan = boards.shape[0], boards.shape[3]
    kin = kernels.shape[2]
    share_width = right_stats.shape[2]
    line = pos * SIDE
    rows = line * SIDE
    chunk = 3 * chan
    ndev = nw * nn
    extra = max(nw.bit_length() - 4, 0)
    dims = (nw, nn, pos, chan)
    hbm = pl.BlockSpec(memory_space=pl.ANY)
    vmem = pl.BlockSpec(memory_space=pltpu.VMEM)
    board_shape = (SIDE, pos, SIDE, chan)

    kept = [
        (2, kin, chan),
        (2, share_width, kin),
        (2, share_width, kin),
        (2, chan, chan),
        (2, chan, chan),
        (2, share_width, chan),
        board_shape,
        board_shape,
        (2, 2, chan),
        (2, 2, chan),
    ]
    arrivals = max(
        sum(room_of(n * chan, kind, extra) for layer, n, kind in PIECES if layer == k)
        for k in range(2)
    )
    flags = sum(len(kind) + 1 + 2 * extra for _, _, kind in PIECES)
    room = (49 + extra) * MIB // 2 + (ndev - 32) * 8 * chan * 4 + 8 * chan * max(arrivals - kin, 0)
    fused = pl.pallas_call(
        functools.partial(fused_kernel, dims),
        out_shape=[pltpu.VMEM(shape, F32) for shape in kept],
        in_specs=[hbm] * 10,
        out_specs=[vmem] * len(kept),
        scratch_shapes=[
            pltpu.VMEM(board_shape, F32),
            pltpu.VMEM(board_shape, F32),
            pltpu.VMEM(history_mask.shape[::-1], jnp.int32),
            pltpu.VMEM((2, 2, chan), F32),
            pltpu.VMEM((2, 2, chan), F32),
            pltpu.VMEM((chan, kin), F32),
            pltpu.VMEM((2, chan, kin), BF16),
            pltpu.VMEM((rows + 2 * line, chunk), BF16),
            pltpu.VMEM((rows + 2 * line, chunk), BF16),
            pltpu.VMEM((rows + 2 * line, chunk), BF16),
            pltpu.VMEM((rows, chan), F32),
            pltpu.VMEM((rows, chan), F32),
            pltpu.VMEM((rows, chan), F32),
            pltpu.VMEM((rows, chan), F32),
            pltpu.VMEM((rows, chan), F32),
            pltpu.VMEM((2, kin, chan), F32),
            pltpu.VMEM((4, ndev, 2, chan), F32),
            pltpu.VMEM((2, arrivals, chan), F32),
            pltpu.SemaphoreType.DMA((13,)),
            pltpu.SemaphoreType.DMA((1,)),
            pltpu.SemaphoreType.DMA((2,)),
            pltpu.SemaphoreType.DMA((2,)),
            pltpu.SemaphoreType.DMA((flags,)),
        ],
        compiler_params=pltpu.CompilerParams(
            collective_id=0, has_side_effects=True, vmem_limit_bytes=room
        ),
        name="fused_passes",
    )
    given = (
        boards,
        history_mask.T,
        kernels,
        norm_params,
        norm_momenta,
        left_stats,
        left_roots,
        jnp.swapaxes(right_stats, 1, 2),
        jnp.swapaxes(right_roots, 1, 2),
        out_cotangent,
    )
    held = fused(*(pltpu.with_memory_space_constraint(v, pltpu.HBM) for v in given))
    held = [pltpu.with_memory_space_constraint(v, pltpu.VMEM) for v in held]
    finish = pl.pallas_call(
        functools.partial(finish_kernel, dims),
        out_shape=[
            pltpu.HBM(boards.shape, F32),
            pltpu.HBM(boards.shape, F32),
            pltpu.HBM((2, share_width, chan), F32),
            pltpu.HBM((2, share_width, chan), F32),
            pltpu.HBM((2, chan, chan), F32),
            pltpu.HBM((2, share_width, kin), F32),
            pltpu.HBM((2, 2, chan), F32),
            pltpu.HBM((2, 2, chan), F32),
        ],
        in_specs=[vmem] * len(kept),
        out_specs=[hbm] * 8,
        scratch_shapes=[
            pltpu.VMEM((kin, chan), BF16),
            pltpu.VMEM((3, share_width, chunk), F32),
            pltpu.VMEM((share_width, chan), F32),
            pltpu.VMEM((chan, chan), F32),
            pltpu.SemaphoreType.DMA((11,)),
        ],
        compiler_params=pltpu.CompilerParams(vmem_limit_bytes=20 * MIB),
        name="finish",
    )
    block_out, board_grad, grad, kernel, left, right, momenta, params = finish(*held)
    return (
        block_out,
        board_grad,
        jnp.swapaxes(grad, 1, 2),
        jnp.swapaxes(kernel, 1, 2),
        left,
        jnp.swapaxes(right, 1, 2),
        momenta,
        params,
    )


def solution(mesh):
    nw, nn = mesh.shape["wide"], mesh.shape["narrow"]
    boards = P(("wide", "narrow"), None, None, None)
    columns = P(None, None, "narrow")
    in_specs = (
        boards,
        P(("wide", "narrow"), None),
        P(),
        P(),
        P(),
        P(),
        columns,
        P(),
        columns,
        boards,
    )
    out_specs = (boards, boards, columns, columns, P(), columns, P(), P())
    return jax.shard_map(
        functools.partial(body, nw, nn),
        mesh=mesh,
        in_specs=in_specs,
        out_specs=out_specs,
        check_vma=False,
    )
```
